32 devices in a mesh: py: 8 (over z, x), pz: 4 (over y, core).
Axes of the slice: x: 2, y: 2, z: 4, core: 2. Of those that a mesh axis runs over, the one named last changes fastest.
Arguments:
- velocity: float32 [3, 288, 160, 2048], P(None, 'pz', 'py'), may hold values from -40 to 40
Outputs:
- filtered_velocity: float32 [3, 32, 16, 256], P(None, None, 'pz', 'py')
- stresses: float32 [6, 32, 16, 256], P(None, None, 'pz', 'py')
The draws below stay inside these ranges and needn't reach their ends.
All inputs are finite; a program needn't handle non-finite values.
Results may differ from the reference program's by a relative error of at most 0.00007.
Values sent between devices are 32-bit elements; how exact they have to be, the bound alone decides.
A program may use at most 192 MiB of HBM per device.

```python
import math
import jax
import jax.numpy as jnp
from jax import lax

NX = 2048
OZ = 32
OX = 256
OY = 16
YIN = 160
ZIN = 288


def draw_velocity(key, part):
    keys = jax.random.split(key, 6)
    shape_full = (3, ZIN, YIN, NX)
    noise = jax.random.truncated_normal(keys[0], -5.0, 5.0, shape_full, jnp.float32)
    x_pos = jnp.arange(NX).astype(jnp.float32)
    y_pos = jnp.arange(YIN).astype(jnp.float32)
    z_pos = jnp.arange(ZIN).astype(jnp.float32)
    waves = jax.random.randint(keys[1], (3, 4, 3), 1, 5).astype(jnp.float32)
    phases = jax.random.uniform(keys[2], (3, 4, 3), jnp.float32, -math.pi, math.pi)
    amplitude = jax.random.uniform(keys[3], (3, 4), jnp.float32, 0.25, 0.5)
    env_waves = jax.random.randint(keys[4], (3,), 1, 4).astype(jnp.float32)
    env_phases = jax.random.uniform(keys[5], (3,), jnp.float32, -math.pi, math.pi)
    two_pi = 2.0 * math.pi
    envelope = jnp.exp(0.5 * (jnp.cos(two_pi * env_waves[0] * x_pos / NX + env_phases[0])[None, None, :] + jnp.cos(two_pi * env_waves[1] * y_pos / 256.0 + env_phases[1])[None, :, None] + jnp.cos(two_pi * env_waves[2] * z_pos / 256.0 + env_phases[2])[:, None, None]))
    components = []
    for comp_index in range(3):
        smooth = jnp.zeros((ZIN, YIN, NX), jnp.float32)
        for mode_index in range(4):
            wave_x = jnp.cos(two_pi * waves[comp_index, mode_index, 0] * x_pos / NX + phases[comp_index, mode_index, 0])
            wave_y = jnp.cos(two_pi * waves[comp_index, mode_index, 1] * y_pos / 256.0 + phases[comp_index, mode_index, 1])
            wave_z = jnp.cos(two_pi * waves[comp_index, mode_index, 2] * z_pos / 256.0 + phases[comp_index, mode_index, 2])
            smooth = smooth + amplitude[comp_index, mode_index] * wave_z[:, None, None] * wave_y[None, :, None] * wave_x[None, None, :]
        rough = noise[comp_index] + 0.6 * noise[(comp_index + 1) % 3]
        components.append(smooth + envelope * rough)
    return jnp.stack(components).astype(jnp.float32)


def setup_inputs(seed: int = 0) -> dict:
    seeds = jax.random.split(jax.random.key(seed), 2)
    velocity = draw_velocity(jax.random.fold_in(seeds[1], 71), 0)
    return dict(velocity=velocity)


spread_cells = 8.0
stress_pairs = ((0, 0), (0, 1), (0, 2), (1, 1), (1, 2), (2, 2))


def gauss_taps():
    offsets = jnp.arange(-16, 17).astype(jnp.float32)
    raw_taps = jnp.exp(-offsets * offsets / (2.0 * spread_cells * spread_cells))
    return raw_taps / jnp.sum(raw_taps)


def reference(velocity):
    taps = gauss_taps()

    def one_plane(plane_index):
        plane = lax.dynamic_index_in_dim(velocity, plane_index, 1, keepdims=False)
        products = jnp.stack([plane[first_comp] * plane[second_comp] for first_comp, second_comp in stress_pairs])
        fields = jnp.concatenate([plane, products], axis=0)
        extended = jnp.concatenate([fields[:, :, NX - 16:], fields, fields[:, :, :16]], axis=2)
        x_sum = jnp.zeros((9, YIN, OX), jnp.float32)
        for offset in range(-16, 17):
            x_sum = x_sum + taps[offset + 16] * extended[:, :, 16 + offset:16 + offset + 8 * OX:8]
        y_sum = jnp.zeros((9, OY, OX), jnp.float32)
        for offset in range(-16, 17):
            y_sum = y_sum + taps[offset + 16] * x_sum[:, 16 + offset:16 + offset + 8 * OY:8, :]
        return y_sum

    stacked = lax.map(one_plane, jnp.arange(ZIN).astype(jnp.int32))
    z_sum = jnp.zeros((OZ, 9, OY, OX), jnp.float32)
    for offset in range(-16, 17):
        z_sum = z_sum + taps[offset + 16] * stacked[16 + offset:16 + offset + 8 * OZ:8]
    filtered = jnp.transpose(z_sum, (1, 0, 2, 3))
    filtered_velocity = filtered[0:3]
    stresses = jnp.stack([filtered[3 + pair_index] - filtered[first_comp] * filtered[second_comp] for pair_index, (first_comp, second_comp) in enumerate(stress_pairs)])
    return filtered_velocity, stresses
```

```python
import functools
import numpy as np
import ml_dtypes
import jax
import jax.numpy as jnp
from jax import lax
from jax.sharding import PartitionSpec as P
from jax.experimental import pallas as pl
from jax.experimental.pallas import tpu as pltpu

stress_pairs = ((0, 0), (0, 1), (0, 2), (1, 1), (1, 2), (2, 2))
f32, bf16 = jnp.float32, jnp.bfloat16


def tap(t):
    r = np.arange(-16, 17).astype(np.float64)
    s = np.sum(np.exp(-r * r / 128.0))
    t = np.asarray(t, np.float64)
    return np.where(np.abs(t) <= 16, np.exp(-t * t / 128.0) / s, 0.0)


class Plan:
    def __init__(self, shape, npy, npz):
        _, self.zl, self.yl, self.nx = shape
        self.npy, self.npz = npy, npz
        zl, yl = self.zl, self.yl
        self.oz = (zl * npz - 32) // 8
        self.oy = (yl * npy - 32) // 8
        self.ox = self.nx // 8
        self.kb = self.ox // npy
        self.jq = self.oy // npz
        self.pk = 128 // self.kb
        self.cz = 8 if zl % 8 == 0 else zl
        self.nch = zl // self.cz
        self.zp = -(-self.cz // 8) * 8
        self.kk = yl * self.zp
        cz, nch = self.cz, self.nch
        base = lambda s: (s + 7) // 8 - 4
        self.base_p = [base(zl * p) for p in range(npz)]
        starts = np.array([[zl * p + cz * c for c in range(nch)] for p in range(npz)])
        bases = base(starts)
        self.nic = int(np.max((starts + cz - 1) // 8 - bases + 1))
        self.offs = bases - bases[:, :1]
        self.ni = int(self.offs.max()) + self.nic
        self.groups = -(-self.ni // self.pk)
        z = starts[:, :, None, None] + np.arange(cz)[None, None, None, :]
        i = bases[:, :, None, None] + np.arange(8)[None, None, :, None]
        az = np.where((i >= 0) & (i < self.oz), tap(z - 16 - 8 * i), 0.0)
        az[:, :, self.nic:] = 0.0
        az = np.pad(az, ((0, 0), (0, 0), (0, 0), (0, self.zp - cz)))
        self.az = np.tile(az, (1, 1, 1, yl)).astype(np.float32)
        ay = np.zeros((npy, 8, yl))
        self.mask = np.zeros((npy, self.oy // 8, 8), np.float32)
        for d in range(npy):
            y = yl * d + np.arange(yl)
            for j in range(self.oy):
                w = tap(y - 16 - 8 * j)
                if np.any(w != 0):
                    ay[d, j % 8] += w
                    self.mask[d, j // 8, j % 8] = 1.0
        assert self.mask.sum(axis=1).max() == 1
        self.ay = np.repeat(ay, self.zp, axis=2).astype(np.float32)
        n = np.arange(self.nx)[:, None]
        k = np.arange(self.ox)[None, :]
        t = (n - 8 * k + self.nx // 2) % self.nx - self.nx // 2
        wx = tap(t).astype(np.float32)
        self.wx_hi = wx.astype(ml_dtypes.bfloat16)
        self.wx_lo = (wx - self.wx_hi.astype(np.float32)).astype(ml_dtypes.bfloat16)


def split(val):
    hi = val.astype(bf16)
    return hi, (val - hi.astype(f32)).astype(bf16)


def dot(a, b):
    return jnp.dot(a, b, preferred_element_type=f32)


def sum_block(pn, c, p, d, v_ref, az_ref, ay_ref, acc):
    xt = 512
    wz = az_ref[p, c][: pn.nic]
    wy = ay_ref[d]
    w = (wz[:, None, :] * wy[None, :, :]).reshape(pn.nic * 8, pn.kk)
    w_hi = w.astype(bf16).astype(f32)
    w2 = jnp.concatenate([w_hi, w - w_hi], axis=0).astype(bf16)
    off = (pn.zl * p + pn.cz * c + 7) // 8 - (pn.zl * p + 7) // 8
    m = pn.nic * 8

    def tile(x, carry):
        xs = pl.ds(pl.multiple_of(x * xt, xt), xt)
        comps = []
        for a in range(3):
            blk = v_ref[a, :, :, xs]
            if pn.zp > pn.cz:
                blk = jnp.concatenate([blk, jnp.zeros((pn.yl, pn.zp - pn.cz, xt), f32)], axis=1)
            comps.append(blk.reshape(pn.kk, xt))
        for f in range(9):
            if f < 3:
                val = comps[f]
            else:
                a, b = stress_pairs[f - 3]
                val = comps[a] * comps[b]
            hi, lo = split(val)
            r = dot(w2, hi) + dot(w2, lo)
            r = (r[:m] + r[m:]).reshape(pn.nic, 8, xt)
            acc[f, pl.ds(off, pn.nic), :, xs] += r
        return carry

    lax.fori_loop(0, pn.nx // xt, tile, 0)


def first_group(pn, g, acc, wh_ref, wl_ref, out_ref):
    rows = min(pn.pk, pn.ni - g * pn.pk)
    parts = []
    for q in range(rows):
        a = acc[:, g * pn.pk + q].reshape(72, pn.nx)
        hi, lo = split(a)
        parts.append(dot(hi, wh_ref[...]) + (dot(lo, wh_ref[...]) + dot(hi, wl_ref[...])))
    lane = lax.broadcasted_iota(jnp.int32, (72, 128), 1)
    for m in range(pn.npy):
        mg, mo = divmod(m * pn.kb, 128)
        res = jnp.zeros((72, 128), f32)
        for q in range(rows):
            piece = parts[q][:, mg * 128:(mg + 1) * 128]
            shift = (q * pn.kb - mo) % 128
            if shift:
                piece = pltpu.roll(piece, shift, 1)
            res = jnp.where((lane >= q * pn.kb) & (lane < (q + 1) * pn.kb), piece, res)
        out_ref[m, g] = res.reshape(9, 8, 128)


def local_kernel(pn, v_ref, az_ref, ay_ref, wh_ref, wl_ref, out_ref, acc):
    c = pl.program_id(0)
    d, p = lax.axis_index("py"), lax.axis_index("pz")

    @pl.when(c == 0)
    def _():
        acc[...] = jnp.zeros_like(acc)

    sum_block(pn, c, p, d, v_ref, az_ref, ay_ref, acc)

    @pl.when(c == pn.nch - 1)
    def _():
        for g in range(pn.groups):
            first_group(pn, g, acc, wh_ref, wl_ref, out_ref)


def local_sums(pn, velocity):
    whole = lambda a: pl.BlockSpec(a.shape, lambda c: (0,) * a.ndim)
    tables = [pn.az, pn.ay, pn.wx_hi, pn.wx_lo]
    return pl.pallas_call(
        functools.partial(local_kernel, pn),
        grid=(pn.nch,),
        in_specs=[pl.BlockSpec((3, pn.yl, pn.cz, pn.nx), lambda c: (0, 0, c, 0))] + [whole(t) for t in tables],
        out_specs=pl.BlockSpec((pn.npy, pn.groups, 9, 8, 128), lambda c: (0, 0, 0, 0, 0)),
        out_shape=jax.ShapeDtypeStruct((pn.npy, pn.groups, 9, 8, 128), f32),
        scratch_shapes=[pltpu.VMEM((9, pn.ni, 8, pn.nx), f32)],
        compiler_params=pltpu.CompilerParams(vmem_limit_bytes=50 * 2**20),
    )(velocity, *[jnp.asarray(t) for t in tables])


def exchange_kernel(pn, in_ref, vel_ref, str_ref, rec_y, snd_z, rec_z, sy, ry, sz, rz):
    d, p = lax.axis_index("py"), lax.axis_index("pz")
    npy, npz, jq, kb = pn.npy, pn.npz, pn.jq, pn.kb
    mesh_id = pl.DeviceIdType.MESH
    barrier = pltpu.get_barrier_semaphore()
    for o in range(1, npy):
        pl.semaphore_signal(barrier, inc=1, device_id=(lax.rem(d + o, npy), p), device_id_type=mesh_id)
    for o in range(1, npz):
        pl.semaphore_signal(barrier, inc=1, device_id=(d, lax.rem(p + o, npz)), device_id_type=mesh_id)
    pl.semaphore_wait(barrier, npy + npz - 2)

    y_copies = []
    for g in range(pn.groups):
        y_copies.append([])
        for o in range(1, npy):
            to = lax.rem(d + o, npy)
            copy = pltpu.make_async_remote_copy(
                src_ref=in_ref.at[to, g], dst_ref=rec_y.at[d, g], send_sem=sy.at[g, o], recv_sem=ry.at[g, o],
                device_id=(to, p), device_id_type=mesh_id)
            copy.start()
            y_copies[g].append(copy)
    rec_y[d] = in_ref[d]
    z_copies = []

    row = lax.broadcasted_iota(jnp.int32, (9, 8, 128), 1)
    for g in range(pn.groups):
        for copy in y_copies[g]:
            copy.wait()
        for h in range(pn.oy // 8):
            total = jnp.zeros((9, 8, 128), f32)
            for s in range(npy):
                rows = np.nonzero(pn.mask[s, h])[0]
                if len(rows) == 0:
                    continue
                val = rec_y[s, g]
                if len(rows) < 8:
                    val = jnp.where((row >= int(rows[0])) & (row <= int(rows[-1])), val, 0.0)
                total = total + val
            for part in range(8 // jq):
                snd_z[h * (8 // jq) + part, g] = total[:, part * jq:(part + 1) * jq, :]
        for o in range(1, npz):
            to = lax.rem(p + o, npz)
            copy = pltpu.make_async_remote_copy(
                src_ref=snd_z.at[to, g], dst_ref=rec_z.at[p, g], send_sem=sz.at[g, o], recv_sem=rz.at[g, o],
                device_id=(d, to), device_id_type=mesh_id)
            copy.start()
            z_copies.append(copy)
    rec_z[p] = snd_z[p]
    for copy in z_copies:
        copy.wait()

    for i in range(pn.oz):
        total = jnp.zeros((9, jq, kb), f32)
        for s in range(npz):
            n = i - pn.base_p[s]
            if 0 <= n < pn.ni:
                g, q = divmod(n, pn.pk)
                total = total + rec_z[s, g, :, :, q * kb:(q + 1) * kb]
        vel_ref[:, i] = total[:3]
        for n, (a, b) in enumerate(stress_pairs):
            str_ref[n, i] = total[3 + n] - total[a] * total[b]


def exchange(pn, packed):
    vmem = pl.BlockSpec(memory_space=pltpu.VMEM)
    zbuf = pltpu.VMEM((pn.npz, pn.groups, 9, pn.jq, 128), f32)
    sems = [pltpu.SemaphoreType.DMA((pn.groups, n)) for n in (pn.npy, pn.npy, pn.npz, pn.npz)]
    return pl.pallas_call(
        functools.partial(exchange_kernel, pn),
        in_specs=[vmem],
        out_specs=(vmem, vmem),
        out_shape=tuple(jax.ShapeDtypeStruct((n, pn.oz, pn.jq, pn.kb), f32) for n in (3, 6)),
        scratch_shapes=[pltpu.VMEM((pn.npy, pn.groups, 9, 8, 128), f32), zbuf, zbuf] + sems,
        compiler_params=pltpu.CompilerParams(
            collective_id=0, has_side_effects=True, vmem_limit_bytes=32 * 2**20
        ),
    )(packed)


class Fast:
    def __init__(self, pn):
        self.npy, self.npz = pn.npy, pn.npz
        npy, npz = pn.npy, pn.npz
        self.xt = pn.nx // npy
        self.kb = pn.kb
        self.own = pn.oz // npz
        self.ok = pn.kb == 32 and pn.oz % npz == 0 and self.own % 4 == 0 and pn.oy % 8 == 0 and pn.oy % npz == 0
        self.ok = self.ok and pn.jq in (4, 8) and npy >= 4 and npz >= 2 and pn.zl % 8 == 0 and pn.mask.sum(axis=1).max() == 1
        if not self.ok:
            return
        self.cz = next(c for c in (24, 16, 8) if pn.zl % c == 0)
        self.nch = pn.zl // self.cz
        self.kk = pn.yl * self.cz
        self.nic = (self.cz - 1) // 8 + 5
        self.groups = self.own // 4 + 2
        self.ng = self.own // 4
        self.slots = self.groups * 4
        first = [(pn.zl * p) // 8 - 4 - (self.own * p - 4) for p in range(npz)]
        self.first = first
        self.step = first[1] - first[0]
        self.ok = all(f == first[0] + self.step * p for p, f in enumerate(first))
        self.ok = self.ok and min(first) >= 0 and max(first) + (self.nch - 1) * self.cz // 8 + self.nic <= self.slots
        if not self.ok:
            return
        z0 = np.array([[pn.zl * p + self.cz * c for c in range(self.nch)] for p in range(npz)])
        z = z0[:, :, None, None] + np.arange(self.cz)
        i = (z0 // 8 - 4)[:, :, None, None] + np.arange(self.nic)[:, None]
        az = np.where((i >= 0) & (i < pn.oz), tap(z - 16 - 8 * i), 0.0)
        az = np.pad(az, ((0, 0), (0, 0), (0, -self.nic % 8), (0, 0)))
        self.az = np.tile(az, (1, 1, 1, pn.yl)).astype(np.float32)
        ay = np.zeros((npy, 8, pn.yl))
        for d in range(npy):
            for j in range(pn.oy):
                w = tap(pn.yl * d + np.arange(pn.yl) - 16 - 8 * j)
                if np.any(w != 0):
                    ay[d, j % 8] += w
        self.ay = np.repeat(ay, self.cz, axis=2).astype(np.float32)
        n = np.arange(self.xt)[:, None]
        k = np.arange(32)[None, :]
        main = tap(n - 8 * k)
        edge = np.where(k >= 16, tap(n - 8 * k + self.xt), tap(n - 8 * k - self.xt))
        wx = np.concatenate([main, edge], axis=1).astype(np.float32)
        hi = wx.astype(ml_dtypes.bfloat16)
        lo = (wx - hi.astype(np.float32)).astype(ml_dtypes.bfloat16)
        t = np.zeros((2, self.xt, 256), ml_dtypes.bfloat16)
        for h in range(2):
            t[0, :, 128 * h:128 * h + 32] = hi[:, 32 * h:32 * h + 32]
            t[0, :, 128 * h + 32:128 * h + 64] = lo[:, 32 * h:32 * h + 32]
            t[1, :, 128 * h:128 * h + 32] = hi[:, 32 * h:32 * h + 32]
        self.wx = t.reshape(2 * self.xt, 256)


def fused_kernel(pn, fs, v_hbm, az_hbm, ay_hbm, wx_hbm, vel_ref, str_ref,
                 vbuf, az, ay, wx, w2, acc, part, rec_h, rec_y, snd_z, rec_z,
                 sv, st, sh, rh, sy, ry, sz, rz):
    d, p = lax.axis_index("py"), lax.axis_index("pz")
    npy, npz, jq, kb = pn.npy, pn.npz, pn.jq, pn.kb
    xt, cz, nch, nic, groups, ng = fs.xt, fs.cz, fs.nch, fs.nic, fs.groups, fs.ng
    mesh_id = pl.DeviceIdType.MESH

    def load(s, c):
        x = pl.multiple_of(lax.rem(d + s, npy) * xt, xt)
        b = lax.rem(s, 2)
        return pltpu.make_async_copy(
            v_hbm.at[:, :, pl.ds(c * cz, cz), pl.ds(x, xt)],
            vbuf.at[b, :, :, pl.ds(c * cz, cz), :], sv.at[b, c])

    tables = [pltpu.make_async_copy(az_hbm.at[p], az, st.at[0]),
              pltpu.make_async_copy(ay_hbm.at[d], ay, st.at[1]),
              pltpu.make_async_copy(wx_hbm, wx, st.at[2])]
    for t in tables:
        t.start()
    for c in range(nch):
        load(0, c).start()

    barrier = pltpu.get_barrier_semaphore()
    for o in range(1, npy):
        pl.semaphore_signal(barrier, inc=1, device_id=(lax.rem(d + o, npy), p), device_id_type=mesh_id)
    for o in range(1, npz):
        pl.semaphore_signal(barrier, inc=1, device_id=(d, lax.rem(p + o, npz)), device_id_type=mesh_id)

    part[...] = jnp.zeros_like(part)
    for t in tables:
        t.wait()
    for c in range(nch):
        wz = az[c][:nic]
        w = (wz[:, None, :] * ay[...][None, :, :]).reshape(nic * 8, fs.kk)
        w_hi = w.astype(bf16)
        w2[c, :nic * 8] = w_hi.astype(f32)
        w2[c, nic * 8:] = w - w_hi.astype(f32)
    pl.semaphore_wait(barrier, npy + npz - 2)

    lane = lax.broadcasted_iota(jnp.int32, (8, 128), 1)
    sub = lax.rem(lane, 32)
    m = nic * 8

    def up(b):
        return pltpu.make_async_remote_copy(
            src_ref=part.at[b, groups - 1], dst_ref=rec_h.at[b, 0], send_sem=sh.at[b, 0], recv_sem=rh.at[b, 0],
            device_id=(d, lax.rem(p + 1, npz)), device_id_type=mesh_id)

    def down(b):
        return pltpu.make_async_remote_copy(
            src_ref=part.at[b, 0], dst_ref=rec_h.at[b, 1], send_sem=sh.at[b, 1], recv_sem=rh.at[b, 1],
            device_id=(d, lax.rem(p + npz - 1, npz)), device_id_type=mesh_id)

    def across(b):
        return pltpu.make_async_remote_copy(
            src_ref=part.at[b, pl.ds(1, ng)], dst_ref=rec_y.at[d], send_sem=sy.at[b], recv_sem=ry.at[b],
            device_id=(lax.rem(d + b, npy), p), device_id_type=mesh_id)

    def halo_start(b):
        @pl.when(p < npz - 1)
        def _():
            up(b).start()

        @pl.when(p > 0)
        def _():
            down(b).start()

    def halo_finish(b):
        @pl.when(p > 0)
        def _():
            up(b).wait_recv()
            part[b, 1] += rec_h[b, 0]

        @pl.when(p < npz - 1)
        def _():
            down(b).wait_recv()
            part[b, ng] += rec_h[b, 1]

    def halo_sent(b):
        @pl.when(p < npz - 1)
        def _():
            up(b).wait_send()

        @pl.when(p > 0)
        def _():
            down(b).wait_send()

    def block(s, carry):
        b = lax.rem(s, 2)

        @pl.when(s < npy - 1)
        def _():
            for c in range(nch):
                load(s + 1, c).start()

        acc[...] = jnp.zeros_like(acc)
        for c in range(nch):
            load(s, c).wait()
            wt = w2[c].astype(bf16)
            row = fs.first[0] + fs.step * p + c * (cz // 8)
            for f in range(9):
                if f < 3:
                    val = vbuf[b, f, :, c * cz:(c + 1) * cz, :]
                else:
                    a1, a2 = stress_pairs[f - 3]
                    val = vbuf[b, a1, :, c * cz:(c + 1) * cz, :] * vbuf[b, a2, :, c * cz:(c + 1) * cz, :]
                hi, lo = split(val.reshape(fs.kk, xt))
                r = dot(wt, hi)
                r = r[:m] + r[m:] + dot(wt[:m], lo)
                acc[f, pl.ds(row, nic)] += r.reshape(nic, 8, xt)

        left, right = lax.rem(s + npy - 1, npy), lax.rem(s + 1, npy)
        for f3 in range(3):
            hi, lo = split(acc[3 * f3:3 * f3 + 3].reshape(3 * fs.slots * 8, xt))
            r = dot(jnp.concatenate([hi, lo], axis=1), wx[...])
            r = r.reshape(3, fs.slots, 8, 256)
            for f in range(3):
                for g in range(groups):
                    pair = []
                    for h in range(2):
                        res = jnp.zeros((8, 128), f32)
                        for q in range(4):
                            piece = r[f, 4 * g + q, :, 128 * h:128 * h + 128]
                            piece = piece + pltpu.roll(piece, 96, 1)
                            if q:
                                piece = pltpu.roll(piece, 32 * q, 1)
                            res = jnp.where((lane >= 32 * q) & (lane < 32 * q + 32), piece, res)
                        pair.append(res)
                    part[s, g, 3 * f3 + f] += pair[0]
                    part[left, g, 3 * f3 + f] += jnp.where(sub >= 16, pair[1], 0.0)
                    part[right, g, 3 * f3 + f] += jnp.where(sub < 16, pair[1], 0.0)

        @pl.when(s >= 3)
        def _():
            halo_finish(s - 2)
            across(s - 2).start()

        @pl.when(s >= 2)
        def _():
            halo_start(s - 1)
        return carry

    lax.fori_loop(0, npy, block, 0)
    halo_start(npy - 1)
    halo_start(0)
    for o in (npy - 2, npy - 1):
        halo_finish(o)
        across(o).start()
    halo_finish(0)
    rec_y[d] = part[0, 1:1 + ng]
    for o in range(1, npy):
        across(o).wait()
    for o in range(npy):
        halo_sent(o)

    rowi = lax.broadcasted_iota(jnp.int32, (ng, 9, 8, 128), 2)
    for h in range(pn.oy // 8):
        total = jnp.zeros((ng, 9, 8, 128), f32)
        for s in range(npy):
            rows = np.nonzero(pn.mask[s, h])[0]
            if len(rows) == 0:
                continue
            val = rec_y[s]
            if len(rows) < 8:
                val = jnp.where((rowi >= int(rows[0])) & (rowi <= int(rows[-1])), val, 0.0)
            total = total + val
        for q in range(8 // jq):
            snd_z[h * (8 // jq) + q] = total[:, :, q * jq:(q + 1) * jq, :]
    copies = []
    for o in range(1, npz):
        to = lax.rem(p + o, npz)
        copy = pltpu.make_async_remote_copy(
            src_ref=snd_z.at[to], dst_ref=rec_z.at[p], send_sem=sz.at[o], recv_sem=rz.at[o],
            device_id=(d, to), device_id_type=mesh_id)
        copy.start()
        copies.append(copy)
    rec_z[p] = snd_z[p]
    for copy in copies:
        copy.wait()
    for s in range(npz):
        for g in range(ng):
            t = rec_z[s, g]
            tau = [t[3 + n] - t[a] * t[b] for n, (a, b) in enumerate(stress_pairs)]
            for q in range(4):
                i = fs.own * s + 4 * g + q
                for n in range(3):
                    vel_ref[n, i] = t[n, :, q * kb:(q + 1) * kb]
                for n in range(6):
                    str_ref[n, i] = tau[n][:, q * kb:(q + 1) * kb]


def fused(pn, fs, velocity):
    vmem = pl.BlockSpec(memory_space=pltpu.VMEM)
    hbm = pl.BlockSpec(memory_space=pl.ANY)
    npy, npz, ng = pn.npy, pn.npz, fs.ng
    dma = lambda *n: pltpu.SemaphoreType.DMA(n)
    return pl.pallas_call(
        functools.partial(fused_kernel, pn, fs),
        in_specs=[hbm] * 4,
        out_specs=(vmem, vmem),
        out_shape=tuple(jax.ShapeDtypeStruct((n, pn.oz, pn.jq, pn.kb), f32) for n in (3, 6)),
        scratch_shapes=[
            pltpu.VMEM((2, 3, pn.yl, pn.zl, fs.xt), f32),
            pltpu.VMEM(fs.az.shape[1:], f32),
            pltpu.VMEM(fs.ay.shape[1:], f32),
            pltpu.VMEM(fs.wx.shape, bf16),
            pltpu.VMEM((fs.nch, 2 * fs.nic * 8, fs.kk), f32),
            pltpu.VMEM((9, fs.slots, 8, fs.xt), f32),
            pltpu.VMEM((npy, fs.groups, 9, 8, 128), f32),
            pltpu.VMEM((npy, 2, 9, 8, 128), f32),
            pltpu.VMEM((npy, ng, 9, 8, 128), f32),
            pltpu.VMEM((npz, ng, 9, pn.jq, 128), f32),
            pltpu.VMEM((npz, ng, 9, pn.jq, 128), f32),
            dma(2, fs.nch), dma(3), dma(npy, 2), dma(npy, 2), dma(npy), dma(npy), dma(npz), dma(npz),
        ],
        compiler_params=pltpu.CompilerParams(
            collective_id=0, has_side_effects=True, vmem_limit_bytes=50 * 2**20
        ),
    )(velocity, *[jnp.asarray(t) for t in (fs.az, fs.ay, fs.wx)])


def on_device(npy, npz, velocity):
    pn = Plan(velocity.shape, npy, npz)
    fs = Fast(pn)
    v = jnp.transpose(velocity, (0, 2, 1, 3))
    if fs.ok:
        return fused(pn, fs, v)
    return exchange(pn, local_sums(pn, v))


def solution(mesh):
    return jax.shard_map(
        functools.partial(on_device, mesh.shape["py"], mesh.shape["pz"]),
        mesh=mesh,
        in_specs=(P(None, "pz", "py", None),),
        out_specs=(P(None, None, "pz", "py"), P(None, None, "pz", "py")),
        check_vma=False,
    )
```

```python
import functools
import numpy as np
import ml_dtypes
import jax
import jax.numpy as jnp
from jax import lax
from jax.sharding import PartitionSpec as P
from jax.experimental import pallas as pl
from jax.experimental.pallas import tpu as pltpu

stress_pairs = ((0, 0), (0, 1), (0, 2), (1, 1), (1, 2), (2, 2))
f32, bf16 = jnp.float32, jnp.bfloat16


def tap(t):
    r = np.arange(-16, 17).astype(np.float64)
    s = np.sum(np.exp(-r * r / 128.0))
    t = np.asarray(t, np.float64)
    return np.where(np.abs(t) <= 16, np.exp(-t * t / 128.0) / s, 0.0)


class Plan:
    def __init__(self, shape, npy, npz):
        _, self.zl, self.yl, self.nx = shape
        self.npy, self.npz = npy, npz
        zl, yl = self.zl, self.yl
        self.oz = (zl * npz - 32) // 8
        self.oy = (yl * npy - 32) // 8
        self.ox = self.nx // 8
        self.kb = self.ox // npy
        self.jq = self.oy // npz
        self.pk = 128 // self.kb
        self.cz = 8 if zl % 8 == 0 else zl
        self.nch = zl // self.cz
        self.zp = -(-self.cz // 8) * 8
        self.kk = yl * self.zp
        cz, nch = self.cz, self.nch
        base = lambda s: (s + 7) // 8 - 4
        self.base_p = [base(zl * p) for p in range(npz)]
        starts = np.array([[zl * p + cz * c for c in range(nch)] for p in range(npz)])
        bases = base(starts)
        self.nic = int(np.max((starts + cz - 1) // 8 - bases + 1))
        self.offs = bases - bases[:, :1]
        self.ni = int(self.offs.max()) + self.nic
        self.groups = -(-self.ni // self.pk)
        z = starts[:, :, None, None] + np.arange(cz)[None, None, None, :]
        i = bases[:, :, None, None] + np.arange(8)[None, None, :, None]
        az = np.where((i >= 0) & (i < self.oz), tap(z - 16 - 8 * i), 0.0)
        az[:, :, self.nic:] = 0.0
        az = np.pad(az, ((0, 0), (0, 0), (0, 0), (0, self.zp - cz)))
        self.az = np.tile(az, (1, 1, 1, yl)).astype(np.float32)
        ay = np.zeros((npy, 8, yl))
        self.mask = np.zeros((npy, self.oy // 8, 8), np.float32)
        for d in range(npy):
            y = yl * d + np.arange(yl)
            for j in range(self.oy):
                w = tap(y - 16 - 8 * j)
                if np.any(w != 0):
                    ay[d, j % 8] += w
                    self.mask[d, j // 8, j % 8] = 1.0
        assert self.mask.sum(axis=1).max() == 1
        self.ay = np.repeat(ay, self.zp, axis=2).astype(np.float32)
        n = np.arange(self.nx)[:, None]
        k = np.arange(self.ox)[None, :]
        t = (n - 8 * k + self.nx // 2) % self.nx - self.nx // 2
        wx = tap(t).astype(np.float32)
        self.wx_hi = wx.astype(ml_dtypes.bfloat16)
        self.wx_lo = (wx - self.wx_hi.astype(np.float32)).astype(ml_dtypes.bfloat16)


def split(val):
    hi = val.astype(bf16)
    return hi, (val - hi.astype(f32)).astype(bf16)


def dot(a, b):
    return jnp.dot(a, b, preferred_element_type=f32)


def sum_block(pn, c, p, d, v_ref, az_ref, ay_ref, acc):
    xt = 512
    wz = az_ref[p, c][: pn.nic]
    wy = ay_ref[d]
    w = (wz[:, None, :] * wy[None, :, :]).reshape(pn.nic * 8, pn.kk)
    w_hi = w.astype(bf16).astype(f32)
    w2 = jnp.concatenate([w_hi, w - w_hi], axis=0).astype(bf16)
    off = (pn.zl * p + pn.cz * c + 7) // 8 - (pn.zl * p + 7) // 8
    m = pn.nic * 8

    def tile(x, carry):
        xs = pl.ds(pl.multiple_of(x * xt, xt), xt)
        comps = []
        for a in range(3):
            blk = v_ref[a, :, :, xs]
            if pn.zp > pn.cz:
                blk = jnp.concatenate([blk, jnp.zeros((pn.yl, pn.zp - pn.cz, xt), f32)], axis=1)
            comps.append(blk.reshape(pn.kk, xt))
        for f in range(9):
            if f < 3:
                val = comps[f]
            else:
                a, b = stress_pairs[f - 3]
                val = comps[a] * comps[b]
            hi, lo = split(val)
            r = dot(w2, hi) + dot(w2, lo)
            r = (r[:m] + r[m:]).reshape(pn.nic, 8, xt)
            acc[f, pl.ds(off, pn.nic), :, xs] += r
        return carry

    lax.fori_loop(0, pn.nx // xt, tile, 0)


def first_group(pn, g, acc, wh_ref, wl_ref, out_ref):
    rows = min(pn.pk, pn.ni - g * pn.pk)
    parts = []
    for q in range(rows):
        a = acc[:, g * pn.pk + q].reshape(72, pn.nx)
        hi, lo = split(a)
        parts.append(dot(hi, wh_ref[...]) + (dot(lo, wh_ref[...]) + dot(hi, wl_ref[...])))
    lane = lax.broadcasted_iota(jnp.int32, (72, 128), 1)
    for m in range(pn.npy):
        mg, mo = divmod(m * pn.kb, 128)
        res = jnp.zeros((72, 128), f32)
        for q in range(rows):
            piece = parts[q][:, mg * 128:(mg + 1) * 128]
            shift = (q * pn.kb - mo) % 128
            if shift:
                piece = pltpu.roll(piece, shift, 1)
            res = jnp.where((lane >= q * pn.kb) & (lane < (q + 1) * pn.kb), piece, res)
        out_ref[m, g] = res.reshape(9, 8, 128)


def local_kernel(pn, v_ref, az_ref, ay_ref, wh_ref, wl_ref, out_ref, acc):
    c = pl.program_id(0)
    d, p = lax.axis_index("py"), lax.axis_index("pz")

    @pl.when(c == 0)
    def _():
        acc[...] = jnp.zeros_like(acc)

    sum_block(pn, c, p, d, v_ref, az_ref, ay_ref, acc)

    @pl.when(c == pn.nch - 1)
    def _():
        for g in range(pn.groups):
            first_group(pn, g, acc, wh_ref, wl_ref, out_ref)


def local_sums(pn, velocity):
    whole = lambda a: pl.BlockSpec(a.shape, lambda c: (0,) * a.ndim)
    tables = [pn.az, pn.ay, pn.wx_hi, pn.wx_lo]
    return pl.pallas_call(
        functools.partial(local_kernel, pn),
        grid=(pn.nch,),
        in_specs=[pl.BlockSpec((3, pn.yl, pn.cz, pn.nx), lambda c: (0, 0, c, 0))] + [whole(t) for t in tables],
        out_specs=pl.BlockSpec((pn.npy, pn.groups, 9, 8, 128), lambda c: (0, 0, 0, 0, 0)),
        out_shape=jax.ShapeDtypeStruct((pn.npy, pn.groups, 9, 8, 128), f32),
        scratch_shapes=[pltpu.VMEM((9, pn.ni, 8, pn.nx), f32)],
        compiler_params=pltpu.CompilerParams(vmem_limit_bytes=50 * 2**20),
    )(velocity, *[jnp.asarray(t) for t in tables])


def exchange_kernel(pn, in_ref, vel_ref, str_ref, rec_y, snd_z, rec_z, sy, ry, sz, rz):
    d, p = lax.axis_index("py"), lax.axis_index("pz")
    npy, npz, jq, kb = pn.npy, pn.npz, pn.jq, pn.kb
    mesh_id = pl.DeviceIdType.MESH
    barrier = pltpu.get_barrier_semaphore()
    for o in range(1, npy):
        pl.semaphore_signal(barrier, inc=1, device_id=(lax.rem(d + o, npy), p), device_id_type=mesh_id)
    for o in range(1, npz):
        pl.semaphore_signal(barrier, inc=1, device_id=(d, lax.rem(p + o, npz)), device_id_type=mesh_id)
    pl.semaphore_wait(barrier, npy + npz - 2)

    y_copies = []
    for g in range(pn.groups):
        y_copies.append([])
        for o in range(1, npy):
            to = lax.rem(d + o, npy)
            copy = pltpu.make_async_remote_copy(
                src_ref=in_ref.at[to, g], dst_ref=rec_y.at[d, g], send_sem=sy.at[g, o], recv_sem=ry.at[g, o],
                device_id=(to, p), device_id_type=mesh_id)
            copy.start()
            y_copies[g].append(copy)
    rec_y[d] = in_ref[d]
    z_copies = []

    row = lax.broadcasted_iota(jnp.int32, (9, 8, 128), 1)
    for g in range(pn.groups):
        for copy in y_copies[g]:
            copy.wait()
        for h in range(pn.oy // 8):
            total = jnp.zeros((9, 8, 128), f32)
            for s in range(npy):
                rows = np.nonzero(pn.mask[s, h])[0]
                if len(rows) == 0:
                    continue
                val = rec_y[s, g]
                if len(rows) < 8:
                    val = jnp.where((row >= int(rows[0])) & (row <= int(rows[-1])), val, 0.0)
                total = total + val
            for part in range(8 // jq):
                snd_z[h * (8 // jq) + part, g] = total[:, part * jq:(part + 1) * jq, :]
        for o in range(1, npz):
            to = lax.rem(p + o, npz)
            copy = pltpu.make_async_remote_copy(
                src_ref=snd_z.at[to, g], dst_ref=rec_z.at[p, g], send_sem=sz.at[g, o], recv_sem=rz.at[g, o],
                device_id=(d, to), device_id_type=mesh_id)
            copy.start()
            z_copies.append(copy)
    rec_z[p] = snd_z[p]
    for copy in z_copies:
        copy.wait()

    for i in range(pn.oz):
        total = jnp.zeros((9, jq, kb), f32)
        for s in range(npz):
            n = i - pn.base_p[s]
            if 0 <= n < pn.ni:
                g, q = divmod(n, pn.pk)
                total = total + rec_z[s, g, :, :, q * kb:(q + 1) * kb]
        vel_ref[:, i] = total[:3]
        for n, (a, b) in enumerate(stress_pairs):
            str_ref[n, i] = total[3 + n] - total[a] * total[b]


def exchange(pn, packed):
    vmem = pl.BlockSpec(memory_space=pltpu.VMEM)
    zbuf = pltpu.VMEM((pn.npz, pn.groups, 9, pn.jq, 128), f32)
    sems = [pltpu.SemaphoreType.DMA((pn.groups, n)) for n in (pn.npy, pn.npy, pn.npz, pn.npz)]
    return pl.pallas_call(
        functools.partial(exchange_kernel, pn),
        in_specs=[vmem],
        out_specs=(vmem, vmem),
        out_shape=tuple(jax.ShapeDtypeStruct((n, pn.oz, pn.jq, pn.kb), f32) for n in (3, 6)),
        scratch_shapes=[pltpu.VMEM((pn.npy, pn.groups, 9, 8, 128), f32), zbuf, zbuf] + sems,
        compiler_params=pltpu.CompilerParams(
            collective_id=0, has_side_effects=True, vmem_limit_bytes=32 * 2**20
        ),
    )(packed)


class Fast:
    def __init__(self, pn):
        self.npy, self.npz = pn.npy, pn.npz
        npy, npz = pn.npy, pn.npz
        self.xt = pn.nx // npy
        self.kb = pn.kb
        self.own = pn.oz // npz
        self.ok = pn.kb == 32 and pn.oz % npz == 0 and self.own % 4 == 0 and pn.oy % 8 == 0 and pn.oy % npz == 0
        self.ok = self.ok and pn.jq in (4, 8) and npy >= 4 and npz >= 2 and pn.zl % 8 == 0 and pn.mask.sum(axis=1).max() == 1
        if not self.ok:
            return
        self.cz = next(c for c in (24, 16, 8) if pn.zl % c == 0)
        self.nch = pn.zl // self.cz
        self.kk = pn.yl * self.cz
        self.nic = (self.cz - 1) // 8 + 5
        self.groups = self.own // 4 + 2
        self.ng = self.own // 4
        self.slots = self.groups * 4
        first = [(pn.zl * p) // 8 - 4 - (self.own * p - 4) for p in range(npz)]
        self.first = first
        self.step = first[1] - first[0]
        self.ok = all(f == first[0] + self.step * p for p, f in enumerate(first))
        self.ok = self.ok and min(first) >= 0 and max(first) + (self.nch - 1) * self.cz // 8 + self.nic <= self.slots
        if not self.ok:
            return
        z0 = np.array([[pn.zl * p + self.cz * c for c in range(self.nch)] for p in range(npz)])
        z = z0[:, :, None, None] + np.arange(self.cz)
        i = (z0 // 8 - 4)[:, :, None, None] + np.arange(self.nic)[:, None]
        az = np.where((i >= 0) & (i < pn.oz), tap(z - 16 - 8 * i), 0.0)
        az = np.pad(az, ((0, 0), (0, 0), (0, -self.nic % 8), (0, 0)))
        self.az = np.tile(az, (1, 1, 1, pn.yl)).astype(np.float32)
        ay = np.zeros((npy, 8, pn.yl))
        for d in range(npy):
            for j in range(pn.oy):
                w = tap(pn.yl * d + np.arange(pn.yl) - 16 - 8 * j)
                if np.any(w != 0):
                    ay[d, j % 8] += w
        self.ay = np.repeat(ay, self.cz, axis=2).astype(np.float32)
        n = np.arange(self.xt)[:, None]
        k = np.arange(32)[None, :]
        main = tap(n - 8 * k)
        edge = np.where(k >= 16, tap(n - 8 * k + self.xt), tap(n - 8 * k - self.xt))
        wx = np.concatenate([main, edge], axis=1).astype(np.float32)
        hi = wx.astype(ml_dtypes.bfloat16)
        lo = (wx - hi.astype(np.float32)).astype(ml_dtypes.bfloat16)
        t = np.zeros((4, 3, self.xt, 2, 4, 32), ml_dtypes.bfloat16)
        for q in range(4):
            for n, val in enumerate((hi, hi, lo)):
                t[q, n, :, :, q] = val.reshape(self.xt, 2, 32)
        self.wx = t.reshape(12 * self.xt, 256)


def fused_kernel(pn, fs, v_hbm, az_hbm, ay_hbm, wx_hbm, vel_ref, str_ref,
                 vbuf, az, ay, wx, w2, acc, part, rec_h, rec_y, snd_z, rec_z,
                 sv, st, sh, rh, sy, ry, sz, rz):
    d, p = lax.axis_index("py"), lax.axis_index("pz")
    npy, npz, jq, kb = pn.npy, pn.npz, pn.jq, pn.kb
    xt, cz, nch, nic, groups, ng = fs.xt, fs.cz, fs.nch, fs.nic, fs.groups, fs.ng
    mesh_id = pl.DeviceIdType.MESH

    def load(s, c):
        x = pl.multiple_of(lax.rem(d + s, npy) * xt, xt)
        b = lax.rem(s, 2)
        return pltpu.make_async_copy(
            v_hbm.at[:, :, pl.ds(c * cz, cz), pl.ds(x, xt)],
            vbuf.at[b, :, :, pl.ds(c * cz, cz), :], sv.at[b, c])

    tables = [pltpu.make_async_copy(az_hbm.at[p], az, st.at[0]),
              pltpu.make_async_copy(ay_hbm.at[d], ay, st.at[1]),
              pltpu.make_async_copy(wx_hbm, wx, st.at[2])]
    for t in tables:
        t.start()
    for c in range(nch):
        load(0, c).start()

    barrier = pltpu.get_barrier_semaphore()
    for o in range(1, npy):
        pl.semaphore_signal(barrier, inc=1, device_id=(lax.rem(d + o, npy), p), device_id_type=mesh_id)
    for o in range(1, npz):
        pl.semaphore_signal(barrier, inc=1, device_id=(d, lax.rem(p + o, npz)), device_id_type=mesh_id)

    part[...] = jnp.zeros_like(part)
    for t in tables:
        t.wait()
    for c in range(nch):
        wz = az[c][:nic]
        w = (wz[:, None, :] * ay[...][None, :, :]).reshape(nic * 8, fs.kk)
        w_hi = w.astype(bf16)
        w2[c, :nic * 8] = w_hi.astype(f32)
        w2[c, nic * 8:] = w - w_hi.astype(f32)
    pl.semaphore_wait(barrier, npy + npz - 2)

    sub = lax.rem(lax.broadcasted_iota(jnp.int32, (groups, 9, 8, 128), 3), 32)
    m = nic * 8

    def up(b):
        return pltpu.make_async_remote_copy(
            src_ref=part.at[b, groups - 1], dst_ref=rec_h.at[b, 0], send_sem=sh.at[b, 0], recv_sem=rh.at[b, 0],
            device_id=(d, lax.rem(p + 1, npz)), device_id_type=mesh_id)

    def down(b):
        return pltpu.make_async_remote_copy(
            src_ref=part.at[b, 0], dst_ref=rec_h.at[b, 1], send_sem=sh.at[b, 1], recv_sem=rh.at[b, 1],
            device_id=(d, lax.rem(p + npz - 1, npz)), device_id_type=mesh_id)

    def across(b):
        return pltpu.make_async_remote_copy(
            src_ref=part.at[b, pl.ds(1, ng)], dst_ref=rec_y.at[d], send_sem=sy.at[b], recv_sem=ry.at[b],
            device_id=(lax.rem(d + b, npy), p), device_id_type=mesh_id)

    def halo_start(b):
        @pl.when(p < npz - 1)
        def _():
            up(b).start()

        @pl.when(p > 0)
        def _():
            down(b).start()

    def halo_finish(b):
        @pl.when(p > 0)
        def _():
            up(b).wait_recv()
            part[b, 1] += rec_h[b, 0]

        @pl.when(p < npz - 1)
        def _():
            down(b).wait_recv()
            part[b, ng] += rec_h[b, 1]

    def halo_sent(b):
        @pl.when(p < npz - 1)
        def _():
            up(b).wait_send()

        @pl.when(p > 0)
        def _():
            down(b).wait_send()

    def block(s, carry):
        b = lax.rem(s, 2)

        @pl.when(s < npy - 1)
        def _():
            for c in range(nch):
                load(s + 1, c).start()

        acc[...] = jnp.zeros_like(acc)
        for c in range(nch):
            load(s, c).wait()
            wt = w2[c].astype(bf16)
            row = fs.first[0] + fs.step * p + c * (cz // 8)
            for f in range(9):
                if f < 3:
                    val = vbuf[b, f, :, c * cz:(c + 1) * cz, :]
                else:
                    a1, a2 = stress_pairs[f - 3]
                    val = vbuf[b, a1, :, c * cz:(c + 1) * cz, :] * vbuf[b, a2, :, c * cz:(c + 1) * cz, :]
                hi, lo = split(val.reshape(fs.kk, xt))
                if f % 2 == 0:
                    r = dot(wt, hi)
                    r = r[:m] + r[m:] + dot(wt[:m], lo)
                else:
                    r_lo = dot(wt[:m], lo)
                    r = dot(wt, hi)
                    r = r[:m] + r[m:] + r_lo
                acc[f, pl.ds(row, nic)] += r.reshape(nic, 8, xt)

        left, right = lax.rem(s + npy - 1, npy), lax.rem(s + 1, npy)
        res = None
        for h in range(2):
            cols = []
            for q in (2 * h, 2 * h + 1):
                a = jnp.concatenate([acc[f, 4 * g + q] for g in range(groups) for f in range(9)], axis=0)
                hi, lo = split(a)
                cols += [hi, lo, hi]
            r = dot(jnp.concatenate(cols, axis=1), wx[6 * xt * h:6 * xt * (h + 1)])
            res = r if res is None else res + r
        main = res[:, :128].reshape(groups, 9, 8, 128)
        edge = res[:, 128:].reshape(groups, 9, 8, 128)
        part[s] += main
        part[left] += jnp.where(sub >= 16, edge, 0.0)
        part[right] += jnp.where(sub < 16, edge, 0.0)

        @pl.when(s >= 3)
        def _():
            halo_finish(s - 2)
            across(s - 2).start()

        @pl.when(s >= 2)
        def _():
            halo_start(s - 1)
        return carry

    lax.fori_loop(0, npy, block, 0)
    halo_start(npy - 1)
    halo_start(0)
    for o in (npy - 2, npy - 1):
        halo_finish(o)
        across(o).start()
    halo_finish(0)
    rec_y[d] = part[0, 1:1 + ng]
    for o in range(1, npy):
        across(o).wait()
    for o in range(npy):
        halo_sent(o)

    rowi = lax.broadcasted_iota(jnp.int32, (ng, 9, 8, 128), 2)
    for h in range(pn.oy // 8):
        total = jnp.zeros((ng, 9, 8, 128), f32)
        for s in range(npy):
            rows = np.nonzero(pn.mask[s, h])[0]
            if len(rows) == 0:
                continue
            val = rec_y[s]
            if len(rows) < 8:
                val = jnp.where((rowi >= int(rows[0])) & (rowi <= int(rows[-1])), val, 0.0)
            total = total + val
        for q in range(8 // jq):
            snd_z[h * (8 // jq) + q] = total[:, :, q * jq:(q + 1) * jq, :]
    copies = []
    for o in range(1, npz):
        to = lax.rem(p + o, npz)
        copy = pltpu.make_async_remote_copy(
            src_ref=snd_z.at[to], dst_ref=rec_z.at[p], send_sem=sz.at[o], recv_sem=rz.at[o],
            device_id=(d, to), device_id_type=mesh_id)
        copy.start()
        copies.append(copy)
    rec_z[p] = snd_z[p]
    for copy in copies:
        copy.wait()
    for s in range(npz):
        for g in range(ng):
            t = rec_z[s, g]
            tau = [t[3 + n] - t[a] * t[b] for n, (a, b) in enumerate(stress_pairs)]
            for q in range(4):
                i = fs.own * s + 4 * g + q
                for n in range(3):
                    vel_ref[n, i] = t[n, :, q * kb:(q + 1) * kb]
                for n in range(6):
                    str_ref[n, i] = tau[n][:, q * kb:(q + 1) * kb]


def fused(pn, fs, velocity):
    vmem = pl.BlockSpec(memory_space=pltpu.VMEM)
    hbm = pl.BlockSpec(memory_space=pltpu.HBM)
    npy, npz, ng = pn.npy, pn.npz, fs.ng
    dma = lambda *n: pltpu.SemaphoreType.DMA(n)
    return pl.pallas_call(
        functools.partial(fused_kernel, pn, fs),
        in_specs=[hbm] * 4,
        out_specs=(vmem, vmem),
        out_shape=tuple(jax.ShapeDtypeStruct((n, pn.oz, pn.jq, pn.kb), f32) for n in (3, 6)),
        scratch_shapes=[
            pltpu.VMEM((2, 3, pn.yl, pn.zl, fs.xt), f32),
            pltpu.VMEM(fs.az.shape[1:], f32),
            pltpu.VMEM(fs.ay.shape[1:], f32),
            pltpu.VMEM(fs.wx.shape, bf16),
            pltpu.VMEM((fs.nch, 2 * fs.nic * 8, fs.kk), f32),
            pltpu.VMEM((9, fs.slots, 8, fs.xt), f32),
            pltpu.VMEM((npy, fs.groups, 9, 8, 128), f32),
            pltpu.VMEM((npy, 2, 9, 8, 128), f32),
            pltpu.VMEM((npy, ng, 9, 8, 128), f32),
            pltpu.VMEM((npz, ng, 9, pn.jq, 128), f32),
            pltpu.VMEM((npz, ng, 9, pn.jq, 128), f32),
            dma(2, fs.nch), dma(3), dma(npy, 2), dma(npy, 2), dma(npy), dma(npy), dma(npz), dma(npz),
        ],
        compiler_params=pltpu.CompilerParams(
            collective_id=0, has_side_effects=True, vmem_limit_bytes=50 * 2**20
        ),
    )(velocity, *[jnp.asarray(t) for t in (fs.az, fs.ay, fs.wx)])


def on_device(npy, npz, velocity):
    pn = Plan(velocity.shape, npy, npz)
    fs = Fast(pn)
    v = jnp.transpose(velocity, (0, 2, 1, 3))
    if fs.ok:
        return fused(pn, fs, v)
    return exchange(pn, local_sums(pn, v))


def solution(mesh):
    return jax.shard_map(
        functools.partial(on_device, mesh.shape["py"], mesh.shape["pz"]),
        mesh=mesh,
        in_specs=(P(None, "pz", "py", None),),
        out_specs=(P(None, None, "pz", "py"), P(None, None, "pz", "py")),
        check_vma=False,
    )
```

```python
import functools
import numpy as np
import ml_dtypes
import jax
import jax.numpy as jnp
from jax import lax
from jax.sharding import PartitionSpec as P
from jax.experimental import pallas as pl
from jax.experimental.pallas import tpu as pltpu

stress_pairs = ((0, 0), (0, 1), (0, 2), (1, 1), (1, 2), (2, 2))
f32, bf16 = jnp.float32, jnp.bfloat16


def tap(t):
    r = np.arange(-16, 17).astype(np.float64)
    s = np.sum(np.exp(-r * r / 128.0))
    t = np.asarray(t, np.float64)
    return np.where(np.abs(t) <= 16, np.exp(-t * t / 128.0) / s, 0.0)


class Plan:
    def __init__(self, shape, npy, npz):
        _, self.zl, self.yl, self.nx = shape
        self.npy, self.npz = npy, npz
        zl, yl = self.zl, self.yl
        self.oz = (zl * npz - 32) // 8
        self.oy = (yl * npy - 32) // 8
        self.ox = self.nx // 8
        self.kb = self.ox // npy
        self.jq = self.oy // npz
        self.pk = 128 // self.kb
        self.cz = 8 if zl % 8 == 0 else zl
        self.nch = zl // self.cz
        self.zp = -(-self.cz // 8) * 8
        self.kk = yl * self.zp
        cz, nch = self.cz, self.nch
        base = lambda s: (s + 7) // 8 - 4
        self.base_p = [base(zl * p) for p in range(npz)]
        starts = np.array([[zl * p + cz * c for c in range(nch)] for p in range(npz)])
        bases = base(starts)
        self.nic = int(np.max((starts + cz - 1) // 8 - bases + 1))
        self.offs = bases - bases[:, :1]
        self.ni = int(self.offs.max()) + self.nic
        self.groups = -(-self.ni // self.pk)
        z = starts[:, :, None, None] + np.arange(cz)[None, None, None, :]
        i = bases[:, :, None, None] + np.arange(8)[None, None, :, None]
        az = np.where((i >= 0) & (i < self.oz), tap(z - 16 - 8 * i), 0.0)
        az[:, :, self.nic:] = 0.0
        az = np.pad(az, ((0, 0), (0, 0), (0, 0), (0, self.zp - cz)))
        self.az = np.tile(az, (1, 1, 1, yl)).astype(np.float32)
        ay = np.zeros((npy, 8, yl))
        self.mask = np.zeros((npy, self.oy // 8, 8), np.float32)
        for d in range(npy):
            y = yl * d + np.arange(yl)
            for j in range(self.oy):
                w = tap(y - 16 - 8 * j)
                if np.any(w != 0):
                    ay[d, j % 8] += w
                    self.mask[d, j // 8, j % 8] = 1.0
        assert self.mask.sum(axis=1).max() == 1
        self.ay = np.repeat(ay, self.zp, axis=2).astype(np.float32)
        n = np.arange(self.nx)[:, None]
        k = np.arange(self.ox)[None, :]
        t = (n - 8 * k + self.nx // 2) % self.nx - self.nx // 2
        wx = tap(t).astype(np.float32)
        self.wx_hi = wx.astype(ml_dtypes.bfloat16)
        self.wx_lo = (wx - self.wx_hi.astype(np.float32)).astype(ml_dtypes.bfloat16)


def split(val):
    hi = val.astype(bf16)
    return hi, (val - hi.astype(f32)).astype(bf16)


def dot(a, b):
    return jnp.dot(a, b, preferred_element_type=f32)


def sum_block(pn, c, p, d, v_ref, az_ref, ay_ref, acc):
    xt = 512
    wz = az_ref[p, c][: pn.nic]
    wy = ay_ref[d]
    w = (wz[:, None, :] * wy[None, :, :]).reshape(pn.nic * 8, pn.kk)
    w_hi = w.astype(bf16).astype(f32)
    w2 = jnp.concatenate([w_hi, w - w_hi], axis=0).astype(bf16)
    off = (pn.zl * p + pn.cz * c + 7) // 8 - (pn.zl * p + 7) // 8
    m = pn.nic * 8

    def tile(x, carry):
        xs = pl.ds(pl.multiple_of(x * xt, xt), xt)
        comps = []
        for a in range(3):
            blk = v_ref[a, :, :, xs]
            if pn.zp > pn.cz:
                blk = jnp.concatenate([blk, jnp.zeros((pn.yl, pn.zp - pn.cz, xt), f32)], axis=1)
            comps.append(blk.reshape(pn.kk, xt))
        for f in range(9):
            if f < 3:
                val = comps[f]
            else:
                a, b = stress_pairs[f - 3]
                val = comps[a] * comps[b]
            hi, lo = split(val)
            r = dot(w2, hi) + dot(w2, lo)
            r = (r[:m] + r[m:]).reshape(pn.nic, 8, xt)
            acc[f, pl.ds(off, pn.nic), :, xs] += r
        return carry

    lax.fori_loop(0, pn.nx // xt, tile, 0)


def first_group(pn, g, acc, wh_ref, wl_ref, out_ref):
    rows = min(pn.pk, pn.ni - g * pn.pk)
    parts = []
    for q in range(rows):
        a = acc[:, g * pn.pk + q].reshape(72, pn.nx)
        hi, lo = split(a)
        parts.append(dot(hi, wh_ref[...]) + (dot(lo, wh_ref[...]) + dot(hi, wl_ref[...])))
    lane = lax.broadcasted_iota(jnp.int32, (72, 128), 1)
    for m in range(pn.npy):
        mg, mo = divmod(m * pn.kb, 128)
        res = jnp.zeros((72, 128), f32)
        for q in range(rows):
            piece = parts[q][:, mg * 128:(mg + 1) * 128]
            shift = (q * pn.kb - mo) % 128
            if shift:
                piece = pltpu.roll(piece, shift, 1)
            res = jnp.where((lane >= q * pn.kb) & (lane < (q + 1) * pn.kb), piece, res)
        out_ref[m, g] = res.reshape(9, 8, 128)


def local_kernel(pn, v_ref, az_ref, ay_ref, wh_ref, wl_ref, out_ref, acc):
    c = pl.program_id(0)
    d, p = lax.axis_index("py"), lax.axis_index("pz")

    @pl.when(c == 0)
    def _():
        acc[...] = jnp.zeros_like(acc)

    sum_block(pn, c, p, d, v_ref, az_ref, ay_ref, acc)

    @pl.when(c == pn.nch - 1)
    def _():
        for g in range(pn.groups):
            first_group(pn, g, acc, wh_ref, wl_ref, out_ref)


def local_sums(pn, velocity):
    whole = lambda a: pl.BlockSpec(a.shape, lambda c: (0,) * a.ndim)
    tables = [pn.az, pn.ay, pn.wx_hi, pn.wx_lo]
    return pl.pallas_call(
        functools.partial(local_kernel, pn),
        grid=(pn.nch,),
        in_specs=[pl.BlockSpec((3, pn.yl, pn.cz, pn.nx), lambda c: (0, 0, c, 0))] + [whole(t) for t in tables],
        out_specs=pl.BlockSpec((pn.npy, pn.groups, 9, 8, 128), lambda c: (0, 0, 0, 0, 0)),
        out_shape=jax.ShapeDtypeStruct((pn.npy, pn.groups, 9, 8, 128), f32),
        scratch_shapes=[pltpu.VMEM((9, pn.ni, 8, pn.nx), f32)],
        compiler_params=pltpu.CompilerParams(vmem_limit_bytes=50 * 2**20),
    )(velocity, *[jnp.asarray(t) for t in tables])


def exchange_kernel(pn, in_ref, vel_ref, str_ref, rec_y, snd_z, rec_z, sy, ry, sz, rz):
    d, p = lax.axis_index("py"), lax.axis_index("pz")
    npy, npz, jq, kb = pn.npy, pn.npz, pn.jq, pn.kb
    mesh_id = pl.DeviceIdType.MESH
    barrier = pltpu.get_barrier_semaphore()
    for o in range(1, npy):
        pl.semaphore_signal(barrier, inc=1, device_id=(lax.rem(d + o, npy), p), device_id_type=mesh_id)
    for o in range(1, npz):
        pl.semaphore_signal(barrier, inc=1, device_id=(d, lax.rem(p + o, npz)), device_id_type=mesh_id)
    pl.semaphore_wait(barrier, npy + npz - 2)

    y_copies = []
    for g in range(pn.groups):
        y_copies.append([])
        for o in range(1, npy):
            to = lax.rem(d + o, npy)
            copy = pltpu.make_async_remote_copy(
                src_ref=in_ref.at[to, g], dst_ref=rec_y.at[d, g], send_sem=sy.at[g, o], recv_sem=ry.at[g, o],
                device_id=(to, p), device_id_type=mesh_id)
            copy.start()
            y_copies[g].append(copy)
    rec_y[d] = in_ref[d]
    z_copies = []

    row = lax.broadcasted_iota(jnp.int32, (9, 8, 128), 1)
    for g in range(pn.groups):
        for copy in y_copies[g]:
            copy.wait()
        for h in range(pn.oy // 8):
            total = jnp.zeros((9, 8, 128), f32)
            for s in range(npy):
                rows = np.nonzero(pn.mask[s, h])[0]
                if len(rows) == 0:
                    continue
                val = rec_y[s, g]
                if len(rows) < 8:
                    val = jnp.where((row >= int(rows[0])) & (row <= int(rows[-1])), val, 0.0)
                total = total + val
            for part in range(8 // jq):
                snd_z[h * (8 // jq) + part, g] = total[:, part * jq:(part + 1) * jq, :]
        for o in range(1, npz):
            to = lax.rem(p + o, npz)
            copy = pltpu.make_async_remote_copy(
                src_ref=snd_z.at[to, g], dst_ref=rec_z.at[p, g], send_sem=sz.at[g, o], recv_sem=rz.at[g, o],
                device_id=(d, to), device_id_type=mesh_id)
            copy.start()
            z_copies.append(copy)
    rec_z[p] = snd_z[p]
    for copy in z_copies:
        copy.wait()

    for i in range(pn.oz):
        total = jnp.zeros((9, jq, kb), f32)
        for s in range(npz):
            n = i - pn.base_p[s]
            if 0 <= n < pn.ni:
                g, q = divmod(n, pn.pk)
                total = total + rec_z[s, g, :, :, q * kb:(q + 1) * kb]
        vel_ref[:, i] = total[:3]
        for n, (a, b) in enumerate(stress_pairs):
            str_ref[n, i] = total[3 + n] - total[a] * total[b]


def exchange(pn, packed):
    vmem = pl.BlockSpec(memory_space=pltpu.VMEM)
    zbuf = pltpu.VMEM((pn.npz, pn.groups, 9, pn.jq, 128), f32)
    sems = [pltpu.SemaphoreType.DMA((pn.groups, n)) for n in (pn.npy, pn.npy, pn.npz, pn.npz)]
    return pl.pallas_call(
        functools.partial(exchange_kernel, pn),
        in_specs=[vmem],
        out_specs=(vmem, vmem),
        out_shape=tuple(jax.ShapeDtypeStruct((n, pn.oz, pn.jq, pn.kb), f32) for n in (3, 6)),
        scratch_shapes=[pltpu.VMEM((pn.npy, pn.groups, 9, 8, 128), f32), zbuf, zbuf] + sems,
        compiler_params=pltpu.CompilerParams(
            collective_id=0, has_side_effects=True, vmem_limit_bytes=32 * 2**20
        ),
    )(packed)


class Fast:
    def __init__(self, pn):
        self.npy, self.npz = pn.npy, pn.npz
        npy, npz = pn.npy, pn.npz
        self.xt = pn.nx // npy
        self.kb = pn.kb
        self.own = pn.oz // npz
        self.ok = pn.kb == 32 and pn.oz % npz == 0 and self.own % 4 == 0 and pn.oy % 8 == 0 and pn.oy % npz == 0
        self.ok = self.ok and pn.jq in (4, 8) and npy >= 4 and npz >= 2 and pn.zl % 8 == 0 and pn.mask.sum(axis=1).max() == 1
        if not self.ok:
            return
        self.cz = next(c for c in (24, 16, 8) if pn.zl % c == 0)
        self.nch = pn.zl // self.cz
        self.kk = pn.yl * self.cz
        self.nic = (self.cz - 1) // 8 + 5
        self.groups = self.own // 4 + 2
        self.ng = self.own // 4
        self.slots = self.groups * 4
        first = [(pn.zl * p) // 8 - 4 - (self.own * p - 4) for p in range(npz)]
        self.first = first
        self.step = first[1] - first[0]
        self.ok = all(f == first[0] + self.step * p for p, f in enumerate(first))
        self.ok = self.ok and min(first) >= 0 and max(first) + (self.nch - 1) * self.cz // 8 + self.nic <= self.slots
        if not self.ok:
            return


def taps(t):
    r = np.arange(-16, 17).astype(np.float64)
    scale = float(1.0 / np.sum(np.exp(-r * r / 128.0)))
    val = jnp.exp((t * t).astype(f32) * (-1.0 / 128.0)) * scale
    return jnp.where((t >= -16) & (t <= 16), val, 0.0)


def weights(pn, fs, d, p, w2, wx):
    iota = lax.broadcasted_iota
    nic, cz, xt = fs.nic, fs.cz, fs.xt
    m = nic * 8
    col = iota(jnp.int32, (8, fs.kk), 1)
    slot = iota(jnp.int32, (8, fs.kk), 0)
    y = jnp.floor((col.astype(f32) + 0.5) * (1.0 / cz)).astype(jnp.int32)
    z = col - y * cz
    wy = jnp.zeros((8, fs.kk), f32)
    for h in range(pn.oy // 8):
        wy = wy + taps(pn.yl * d + y - 16 - 8 * (slot + 8 * h))
    wz0 = taps(z + 16 - 8 * slot)
    for c in range(fs.nch):
        i = (pn.zl * p + cz * c) // 8 - 4 + slot
        wz = jnp.where((i >= 0) & (i < pn.oz), wz0, 0.0)[:nic]
        w = (wz[:, None, :] * wy[None, :, :]).reshape(m, fs.kk)
        w_hi = w.astype(bf16).astype(f32)
        w2[c, :m] = w_hi
        w2[c, m:] = w - w_hi
    row = iota(jnp.int32, (xt, 128), 0)
    lane = iota(jnp.int32, (xt, 128), 1)
    k = lane & 31
    t = row - 8 * k
    main = taps(t)
    edge = taps(jnp.where(k >= 16, t + xt, t - xt))
    for q in range(4):
        here = (lane >> 5) == q
        val = jnp.concatenate([jnp.where(here, main, 0.0), jnp.where(here, edge, 0.0)], axis=1)
        hi, lo = split(val)
        for n, part in enumerate((hi, hi, lo)):
            wx[(3 * q + n) * xt:(3 * q + n + 1) * xt] = part


def fused_kernel(pn, fs, v_hbm, vel_ref, str_ref,
                 vbuf, wx, w2, acc, part, rec_h, rec_d, rec_y, snd_z, rec_z,
                 sv, sh, rh, sd, rd, sy, ry, sz, rz):
    d, p = lax.axis_index("py"), lax.axis_index("pz")
    npy, npz, jq, kb = pn.npy, pn.npz, pn.jq, pn.kb
    xt, cz, nch, nic, groups, ng = fs.xt, fs.cz, fs.nch, fs.nic, fs.groups, fs.ng
    mesh_id = pl.DeviceIdType.MESH

    def load(s, c):
        x = pl.multiple_of(lax.rem(d + s, npy) * xt, xt)
        b = lax.rem(s, 2)
        return pltpu.make_async_copy(
            v_hbm.at[:, :, pl.ds(c * cz, cz), pl.ds(x, xt)],
            vbuf.at[b, :, :, pl.ds(c * cz, cz), :], sv.at[b, c])

    for c in range(nch):
        load(0, c).start()

    barrier = pltpu.get_barrier_semaphore()
    for o in range(1, npy * npz):
        od, op = divmod(o, npz)
        to = (lax.rem(d + od, npy), lax.rem(p + op, npz))
        pl.semaphore_signal(barrier, inc=1, device_id=to, device_id_type=mesh_id)

    part[...] = jnp.zeros_like(part)
    weights(pn, fs, d, p, w2, wx)

    sub = lax.rem(lax.broadcasted_iota(jnp.int32, (groups, 9, 8, 128), 3), 32)
    m = nic * 8

    def up(b):
        return pltpu.make_async_remote_copy(
            src_ref=part.at[b, groups - 1], dst_ref=rec_h.at[b, 0], send_sem=sh.at[b, 0], recv_sem=rh.at[b, 0],
            device_id=(d, lax.rem(p + 1, npz)), device_id_type=mesh_id)

    def down(b):
        return pltpu.make_async_remote_copy(
            src_ref=part.at[b, 0], dst_ref=rec_h.at[b, 1], send_sem=sh.at[b, 1], recv_sem=rh.at[b, 1],
            device_id=(d, lax.rem(p + npz - 1, npz)), device_id_type=mesh_id)

    def across(b):
        return pltpu.make_async_remote_copy(
            src_ref=part.at[b, pl.ds(1, ng)], dst_ref=rec_y.at[d], send_sem=sy.at[b], recv_sem=ry.at[b],
            device_id=(lax.rem(d + b, npy), p), device_id_type=mesh_id)

    def slant(b, k):
        o = b - (npy - 2)
        to = (lax.rem(d + b, npy), lax.rem(p + (1 if k == 0 else npz - 1), npz))
        return pltpu.make_async_remote_copy(
            src_ref=part.at[b, groups - 1 if k == 0 else 0], dst_ref=rec_d.at[o, k], send_sem=sd.at[o, k],
            recv_sem=rd.at[o, k], device_id=to, device_id_type=mesh_id)

    def halo_start(b):
        @pl.when(p < npz - 1)
        def _():
            up(b).start()

        @pl.when(p > 0)
        def _():
            down(b).start()

    def halo_finish(b):
        @pl.when(p > 0)
        def _():
            up(b).wait_recv()
            part[b, 1] += rec_h[b, 0]

        @pl.when(p < npz - 1)
        def _():
            down(b).wait_recv()
            part[b, ng] += rec_h[b, 1]

    def halo_sent(b):
        @pl.when(p < npz - 1)
        def _():
            up(b).wait_send()

        @pl.when(p > 0)
        def _():
            down(b).wait_send()

    def block(s, carry):
        b = lax.rem(s, 2)

        @pl.when(s < npy - 1)
        def _():
            for c in range(nch):
                load(s + 1, c).start()

        acc[...] = jnp.zeros_like(acc)
        for c in range(nch):
            load(s, c).wait()
            wt = w2[c].astype(bf16)
            row = fs.first[0] + fs.step * p + c * (cz // 8)
            for f in range(9):
                if f < 3:
                    val = vbuf[b, f, :, c * cz:(c + 1) * cz, :]
                else:
                    a1, a2 = stress_pairs[f - 3]
                    val = vbuf[b, a1, :, c * cz:(c + 1) * cz, :] * vbuf[b, a2, :, c * cz:(c + 1) * cz, :]
                hi, lo = split(val.reshape(fs.kk, xt))
                if f % 2 == 0:
                    r = dot(wt, hi)
                    r = r[:m] + r[m:] + dot(wt[:m], lo)
                else:
                    r_lo = dot(wt[:m], lo)
                    r = dot(wt, hi)
                    r = r[:m] + r[m:] + r_lo
                acc[f, pl.ds(row, nic)] += r.reshape(nic, 8, xt)

        left, right = lax.rem(s + npy - 1, npy), lax.rem(s + 1, npy)
        res = None
        for h in range(2):
            cols = []
            for q in (2 * h, 2 * h + 1):
                a = jnp.concatenate([acc[f, 4 * g + q] for g in range(groups) for f in range(9)], axis=0)
                hi, lo = split(a)
                cols += [hi, lo, hi]
            r = dot(jnp.concatenate(cols, axis=1), wx[6 * xt * h:6 * xt * (h + 1)])
            res = r if res is None else res + r
        main = res[:, :128].reshape(groups, 9, 8, 128)
        edge = res[:, 128:].reshape(groups, 9, 8, 128)
        part[s] += main
        part[left] += jnp.where(sub >= 16, edge, 0.0)
        part[right] += jnp.where(sub < 16, edge, 0.0)

        @pl.when(s == 1)
        def _():
            pl.semaphore_wait(barrier, npy * npz - 1)

        @pl.when(s >= 3)
        def _():
            halo_finish(s - 2)
            across(s - 2).start()

        @pl.when((s >= 2) & (s <= npy - 2))
        def _():
            halo_start(s - 1)
        return carry

    lax.fori_loop(0, npy, block, 0)
    late = [(o, k) for o in (npy - 2, npy - 1) for k in range(2)]
    for o in (npy - 2, npy - 1):
        across(o).start()
    for o, k in late:
        @pl.when((p < npz - 1) if k == 0 else (p > 0))
        def _():
            slant(o, k).start()
    halo_start(0)
    halo_finish(0)
    rec_y[d] = part[0, 1:1 + ng]
    for o in range(1, npy):
        across(o).wait()
    for o, k in late:
        @pl.when((p > 0) if k == 0 else (p < npz - 1))
        def _():
            slant(o, k).wait_recv()
            rec_y[lax.rem(d + npy - o, npy), 0 if k == 0 else ng - 1] += rec_d[o - (npy - 2), k]

    rowi = lax.broadcasted_iota(jnp.int32, (ng, 9, 8, 128), 2)
    for h in range(pn.oy // 8):
        total = jnp.zeros((ng, 9, 8, 128), f32)
        for s in range(npy):
            rows = np.nonzero(pn.mask[s, h])[0]
            if len(rows) == 0:
                continue
            val = rec_y[s]
            if len(rows) < 8:
                val = jnp.where((rowi >= int(rows[0])) & (rowi <= int(rows[-1])), val, 0.0)
            total = total + val
        for q in range(8 // jq):
            snd_z[h * (8 // jq) + q] = total[:, :, q * jq:(q + 1) * jq, :]
    copies = []
    for o in range(1, npz):
        to = lax.rem(p + o, npz)
        copy = pltpu.make_async_remote_copy(
            src_ref=snd_z.at[to], dst_ref=rec_z.at[p], send_sem=sz.at[o], recv_sem=rz.at[o],
            device_id=(d, to), device_id_type=mesh_id)
        copy.start()
        copies.append(copy)
    rec_z[p] = snd_z[p]
    for copy in copies:
        copy.wait()
    for o in range(npy - 2):
        halo_sent(o)
    for o, k in late:
        @pl.when((p < npz - 1) if k == 0 else (p > 0))
        def _():
            slant(o, k).wait_send()
    for s in range(npz):
        for g in range(ng):
            t = rec_z[s, g]
            tau = [t[3 + n] - t[a] * t[b] for n, (a, b) in enumerate(stress_pairs)]
            for q in range(4):
                i = fs.own * s + 4 * g + q
                for n in range(3):
                    vel_ref[n, i] = t[n, :, q * kb:(q + 1) * kb]
                for n in range(6):
                    str_ref[n, i] = tau[n][:, q * kb:(q + 1) * kb]


def fused(pn, fs, velocity):
    vmem = pl.BlockSpec(memory_space=pltpu.VMEM)
    hbm = pl.BlockSpec(memory_space=pltpu.HBM)
    npy, npz, ng = pn.npy, pn.npz, fs.ng
    dma = lambda *n: pltpu.SemaphoreType.DMA(n)
    return pl.pallas_call(
        functools.partial(fused_kernel, pn, fs),
        in_specs=[hbm],
        out_specs=(vmem, vmem),
        out_shape=tuple(jax.ShapeDtypeStruct((n, pn.oz, pn.jq, pn.kb), f32) for n in (3, 6)),
        scratch_shapes=[
            pltpu.VMEM((2, 3, pn.yl, pn.zl, fs.xt), f32),
            pltpu.VMEM((12 * fs.xt, 256), bf16),
            pltpu.VMEM((fs.nch, 2 * fs.nic * 8, fs.kk), f32),
            pltpu.VMEM((9, fs.slots, 8, fs.xt), f32),
            pltpu.VMEM((npy, fs.groups, 9, 8, 128), f32),
            pltpu.VMEM((npy, 2, 9, 8, 128), f32),
            pltpu.VMEM((2, 2, 9, 8, 128), f32),
            pltpu.VMEM((npy, ng, 9, 8, 128), f32),
            pltpu.VMEM((npz, ng, 9, pn.jq, 128), f32),
            pltpu.VMEM((npz, ng, 9, pn.jq, 128), f32),
            dma(2, fs.nch), dma(npy, 2), dma(npy, 2), dma(2, 2), dma(2, 2), dma(npy), dma(npy), dma(npz), dma(npz),
        ],
        compiler_params=pltpu.CompilerParams(
            collective_id=0, has_side_effects=True, vmem_limit_bytes=50 * 2**20
        ),
    )(velocity)


def on_device(npy, npz, velocity):
    pn = Plan(velocity.shape, npy, npz)
    fs = Fast(pn)
    v = jnp.transpose(velocity, (0, 2, 1, 3))
    if fs.ok:
        return fused(pn, fs, v)
    return exchange(pn, local_sums(pn, v))


def solution(mesh):
    return jax.shard_map(
        functools.partial(on_device, mesh.shape["py"], mesh.shape["pz"]),
        mesh=mesh,
        in_specs=(P(None, "pz", "py", None),),
        out_specs=(P(None, None, "pz", "py"), P(None, None, "pz", "py")),
        check_vma=False,
    )
```

```python
import functools
import numpy as np
import ml_dtypes
import jax
import jax.numpy as jnp
from jax import lax
from jax.sharding import PartitionSpec as P
from jax.experimental import pallas as pl
from jax.experimental.pallas import tpu as pltpu

stress_pairs = ((0, 0), (0, 1), (0, 2), (1, 1), (1, 2), (2, 2))
f32, bf16 = jnp.float32, jnp.bfloat16


def tap(t):
    r = np.arange(-16, 17).astype(np.float64)
    s = np.sum(np.exp(-r * r / 128.0))
    t = np.asarray(t, np.float64)
    return np.where(np.abs(t) <= 16, np.exp(-t * t / 128.0) / s, 0.0)


class Plan:
    def __init__(self, shape, npy, npz):
        _, self.zl, self.yl, self.nx = shape
        self.npy, self.npz = npy, npz
        zl, yl = self.zl, self.yl
        self.oz = (zl * npz - 32) // 8
        self.oy = (yl * npy - 32) // 8
        self.ox = self.nx // 8
        self.kb = self.ox // npy
        self.jq = self.oy // npz
        self.pk = 128 // self.kb
        self.cz = 8 if zl % 8 == 0 else zl
        self.nch = zl // self.cz
        self.zp = -(-self.cz // 8) * 8
        self.kk = yl * self.zp
        cz, nch = self.cz, self.nch
        base = lambda s: (s + 7) // 8 - 4
        self.base_p = [base(zl * p) for p in range(npz)]
        starts = np.array([[zl * p + cz * c for c in range(nch)] for p in range(npz)])
        bases = base(starts)
        self.nic = int(np.max((starts + cz - 1) // 8 - bases + 1))
        self.offs = bases - bases[:, :1]
        self.ni = int(self.offs.max()) + self.nic
        self.groups = -(-self.ni // self.pk)
        z = starts[:, :, None, None] + np.arange(cz)[None, None, None, :]
        i = bases[:, :, None, None] + np.arange(8)[None, None, :, None]
        az = np.where((i >= 0) & (i < self.oz), tap(z - 16 - 8 * i), 0.0)
        az[:, :, self.nic:] = 0.0
        az = np.pad(az, ((0, 0), (0, 0), (0, 0), (0, self.zp - cz)))
        self.az = np.tile(az, (1, 1, 1, yl)).astype(np.float32)
        ay = np.zeros((npy, 8, yl))
        self.mask = np.zeros((npy, self.oy // 8, 8), np.float32)
        for d in range(npy):
            y = yl * d + np.arange(yl)
            for j in range(self.oy):
                w = tap(y - 16 - 8 * j)
                if np.any(w != 0):
                    ay[d, j % 8] += w
                    self.mask[d, j // 8, j % 8] = 1.0
        assert self.mask.sum(axis=1).max() == 1
        self.ay = np.repeat(ay, self.zp, axis=2).astype(np.float32)
        n = np.arange(self.nx)[:, None]
        k = np.arange(self.ox)[None, :]
        t = (n - 8 * k + self.nx // 2) % self.nx - self.nx // 2
        wx = tap(t).astype(np.float32)
        self.wx_hi = wx.astype(ml_dtypes.bfloat16)
        self.wx_lo = (wx - self.wx_hi.astype(np.float32)).astype(ml_dtypes.bfloat16)


def split(val):
    hi = val.astype(bf16)
    return hi, (val - hi.astype(f32)).astype(bf16)


def dot(a, b):
    return jnp.dot(a, b, preferred_element_type=f32)


def sum_block(pn, c, p, d, v_ref, az_ref, ay_ref, acc):
    xt = 512
    wz = az_ref[p, c][: pn.nic]
    wy = ay_ref[d]
    w = (wz[:, None, :] * wy[None, :, :]).reshape(pn.nic * 8, pn.kk)
    w_hi = w.astype(bf16).astype(f32)
    w2 = jnp.concatenate([w_hi, w - w_hi], axis=0).astype(bf16)
    off = (pn.zl * p + pn.cz * c + 7) // 8 - (pn.zl * p + 7) // 8
    m = pn.nic * 8

    def tile(x, carry):
        xs = pl.ds(pl.multiple_of(x * xt, xt), xt)
        comps = []
        for a in range(3):
            blk = v_ref[a, :, :, xs]
            if pn.zp > pn.cz:
                blk = jnp.concatenate([blk, jnp.zeros((pn.yl, pn.zp - pn.cz, xt), f32)], axis=1)
            comps.append(blk.reshape(pn.kk, xt))
        for f in range(9):
            if f < 3:
                val = comps[f]
            else:
                a, b = stress_pairs[f - 3]
                val = comps[a] * comps[b]
            hi, lo = split(val)
            r = dot(w2, hi) + dot(w2, lo)
            r = (r[:m] + r[m:]).reshape(pn.nic, 8, xt)
            acc[f, pl.ds(off, pn.nic), :, xs] += r
        return carry

    lax.fori_loop(0, pn.nx // xt, tile, 0)


def first_group(pn, g, acc, wh_ref, wl_ref, out_ref):
    rows = min(pn.pk, pn.ni - g * pn.pk)
    parts = []
    for q in range(rows):
        a = acc[:, g * pn.pk + q].reshape(72, pn.nx)
        hi, lo = split(a)
        parts.append(dot(hi, wh_ref[...]) + (dot(lo, wh_ref[...]) + dot(hi, wl_ref[...])))
    lane = lax.broadcasted_iota(jnp.int32, (72, 128), 1)
    for m in range(pn.npy):
        mg, mo = divmod(m * pn.kb, 128)
        res = jnp.zeros((72, 128), f32)
        for q in range(rows):
            piece = parts[q][:, mg * 128:(mg + 1) * 128]
            shift = (q * pn.kb - mo) % 128
            if shift:
                piece = pltpu.roll(piece, shift, 1)
            res = jnp.where((lane >= q * pn.kb) & (lane < (q + 1) * pn.kb), piece, res)
        out_ref[m, g] = res.reshape(9, 8, 128)


def local_kernel(pn, v_ref, az_ref, ay_ref, wh_ref, wl_ref, out_ref, acc):
    c = pl.program_id(0)
    d, p = lax.axis_index("py"), lax.axis_index("pz")

    @pl.when(c == 0)
    def _():
        acc[...] = jnp.zeros_like(acc)

    sum_block(pn, c, p, d, v_ref, az_ref, ay_ref, acc)

    @pl.when(c == pn.nch - 1)
    def _():
        for g in range(pn.groups):
            first_group(pn, g, acc, wh_ref, wl_ref, out_ref)


def local_sums(pn, velocity):
    whole = lambda a: pl.BlockSpec(a.shape, lambda c: (0,) * a.ndim)
    tables = [pn.az, pn.ay, pn.wx_hi, pn.wx_lo]
    return pl.pallas_call(
        functools.partial(local_kernel, pn),
        grid=(pn.nch,),
        in_specs=[pl.BlockSpec((3, pn.yl, pn.cz, pn.nx), lambda c: (0, 0, c, 0))] + [whole(t) for t in tables],
        out_specs=pl.BlockSpec((pn.npy, pn.groups, 9, 8, 128), lambda c: (0, 0, 0, 0, 0)),
        out_shape=jax.ShapeDtypeStruct((pn.npy, pn.groups, 9, 8, 128), f32),
        scratch_shapes=[pltpu.VMEM((9, pn.ni, 8, pn.nx), f32)],
        compiler_params=pltpu.CompilerParams(vmem_limit_bytes=50 * 2**20),
    )(velocity, *[jnp.asarray(t) for t in tables])


def exchange_kernel(pn, in_ref, vel_ref, str_ref, rec_y, snd_z, rec_z, sy, ry, sz, rz):
    d, p = lax.axis_index("py"), lax.axis_index("pz")
    npy, npz, jq, kb = pn.npy, pn.npz, pn.jq, pn.kb
    mesh_id = pl.DeviceIdType.MESH
    barrier = pltpu.get_barrier_semaphore()
    for o in range(1, npy):
        pl.semaphore_signal(barrier, inc=1, device_id=(lax.rem(d + o, npy), p), device_id_type=mesh_id)
    for o in range(1, npz):
        pl.semaphore_signal(barrier, inc=1, device_id=(d, lax.rem(p + o, npz)), device_id_type=mesh_id)
    pl.semaphore_wait(barrier, npy + npz - 2)

    y_copies = []
    for g in range(pn.groups):
        y_copies.append([])
        for o in range(1, npy):
            to = lax.rem(d + o, npy)
            copy = pltpu.make_async_remote_copy(
                src_ref=in_ref.at[to, g], dst_ref=rec_y.at[d, g], send_sem=sy.at[g, o], recv_sem=ry.at[g, o],
                device_id=(to, p), device_id_type=mesh_id)
            copy.start()
            y_copies[g].append(copy)
    rec_y[d] = in_ref[d]
    z_copies = []

    row = lax.broadcasted_iota(jnp.int32, (9, 8, 128), 1)
    for g in range(pn.groups):
        for copy in y_copies[g]:
            copy.wait()
        for h in range(pn.oy // 8):
            total = jnp.zeros((9, 8, 128), f32)
            for s in range(npy):
                rows = np.nonzero(pn.mask[s, h])[0]
                if len(rows) == 0:
                    continue
                val = rec_y[s, g]
                if len(rows) < 8:
                    val = jnp.where((row >= int(rows[0])) & (row <= int(rows[-1])), val, 0.0)
                total = total + val
            for part in range(8 // jq):
                snd_z[h * (8 // jq) + part, g] = total[:, part * jq:(part + 1) * jq, :]
        for o in range(1, npz):
            to = lax.rem(p + o, npz)
            copy = pltpu.make_async_remote_copy(
                src_ref=snd_z.at[to, g], dst_ref=rec_z.at[p, g], send_sem=sz.at[g, o], recv_sem=rz.at[g, o],
                device_id=(d, to), device_id_type=mesh_id)
            copy.start()
            z_copies.append(copy)
    rec_z[p] = snd_z[p]
    for copy in z_copies:
        copy.wait()

    for i in range(pn.oz):
        total = jnp.zeros((9, jq, kb), f32)
        for s in range(npz):
            n = i - pn.base_p[s]
            if 0 <= n < pn.ni:
                g, q = divmod(n, pn.pk)
                total = total + rec_z[s, g, :, :, q * kb:(q + 1) * kb]
        vel_ref[:, i] = total[:3]
        for n, (a, b) in enumerate(stress_pairs):
            str_ref[n, i] = total[3 + n] - total[a] * total[b]


def exchange(pn, packed):
    vmem = pl.BlockSpec(memory_space=pltpu.VMEM)
    zbuf = pltpu.VMEM((pn.npz, pn.groups, 9, pn.jq, 128), f32)
    sems = [pltpu.SemaphoreType.DMA((pn.groups, n)) for n in (pn.npy, pn.npy, pn.npz, pn.npz)]
    return pl.pallas_call(
        functools.partial(exchange_kernel, pn),
        in_specs=[vmem],
        out_specs=(vmem, vmem),
        out_shape=tuple(jax.ShapeDtypeStruct((n, pn.oz, pn.jq, pn.kb), f32) for n in (3, 6)),
        scratch_shapes=[pltpu.VMEM((pn.npy, pn.groups, 9, 8, 128), f32), zbuf, zbuf] + sems,
        compiler_params=pltpu.CompilerParams(
            collective_id=0, has_side_effects=True, vmem_limit_bytes=32 * 2**20
        ),
    )(packed)


class Fast:
    def __init__(self, pn):
        self.npy, self.npz = pn.npy, pn.npz
        npy, npz = pn.npy, pn.npz
        self.xt = pn.nx // npy
        self.kb = pn.kb
        self.own = pn.oz // npz
        self.ok = pn.kb == 32 and pn.oz % npz == 0 and self.own % 4 == 0 and pn.oy % 8 == 0 and pn.oy % npz == 0
        self.ok = self.ok and pn.jq in (4, 8) and npy >= 4 and npz >= 2 and pn.zl % 8 == 0 and pn.mask.sum(axis=1).max() == 1
        if not self.ok:
            return
        self.cz = next(c for c in (24, 16, 8) if pn.zl % c == 0)
        self.nch = pn.zl // self.cz
        self.kk = pn.yl * self.cz
        self.nic = (self.cz - 1) // 8 + 5
        self.groups = self.own // 4 + 2
        self.ng = self.own // 4
        self.slots = self.groups * 4
        first = [(pn.zl * p) // 8 - 4 - (self.own * p - 4) for p in range(npz)]
        self.first = first
        self.step = first[1] - first[0]
        self.ok = all(f == first[0] + self.step * p for p, f in enumerate(first))
        y0 = pn.yl * np.arange(npy)
        self.jlo = [int(max(0, (y + 7) // 8 - 4)) for y in y0]
        self.rows = [int(min(pn.oy - 1, (y + pn.yl - 1) // 8)) - j + 1 for y, j in zip(y0, self.jlo)]
        self.sent = [min(8, n | 1) for n in self.rows]
        self.ok = self.ok and 0 < min(self.rows) and max(self.rows) <= 8 and min(first) >= 0 and max(first) + (self.nch - 1) * self.cz // 8 + self.nic <= self.slots
        if not self.ok:
            return


def taps(t):
    r = np.arange(-16, 17).astype(np.float64)
    scale = float(1.0 / np.sum(np.exp(-r * r / 128.0)))
    val = jnp.exp((t * t).astype(f32) * (-1.0 / 128.0)) * scale
    return jnp.where((t >= -16) & (t <= 16), val, 0.0)


def weights(pn, fs, d, p, w2, wx):
    iota = lax.broadcasted_iota
    nic, cz, xt = fs.nic, fs.cz, fs.xt
    m = nic * 8
    col = iota(jnp.int32, (8, fs.kk), 1)
    slot = iota(jnp.int32, (8, fs.kk), 0)
    y = jnp.floor((col.astype(f32) + 0.5) * (1.0 / cz)).astype(jnp.int32)
    z = col - y * cz
    j = jnp.maximum((pn.yl * d + 7) // 8 - 4, 0) + slot
    wy = jnp.where(j < pn.oy, taps(pn.yl * d + y - 16 - 8 * j), 0.0)
    wz0 = taps(z + 16 - 8 * slot)
    for c in range(fs.nch):
        i = (pn.zl * p + cz * c) // 8 - 4 + slot
        wz = jnp.where((i >= 0) & (i < pn.oz), wz0, 0.0)[:nic]
        w = (wz[:, None, :] * wy[None, :, :]).reshape(m, fs.kk)
        w_hi = w.astype(bf16).astype(f32)
        w2[c, :m] = w_hi
        w2[c, m:] = w - w_hi
    row = iota(jnp.int32, (xt, 128), 0)
    lane = iota(jnp.int32, (xt, 128), 1)
    k = lane & 31
    t = row - 8 * k
    main = taps(t)
    edge = taps(jnp.where(k >= 16, t + xt, t - xt))
    for q in range(4):
        here = (lane >> 5) == q
        val = jnp.concatenate([jnp.where(here, main, 0.0), jnp.where(here, edge, 0.0)], axis=1)
        hi, lo = split(val)
        for n, part in enumerate((hi, hi, lo)):
            wx[(3 * q + n) * xt:(3 * q + n + 1) * xt] = part


def fused_kernel(pn, fs, v_hbm, vel_ref, str_ref,
                 vbuf, wx, w2, acc, part, rec_h, rec_d, rec_y, tot, snd_z, rec_z,
                 sv, sh, rh, sd, rd, sy, ry, sz, rz):
    d, p = lax.axis_index("py"), lax.axis_index("pz")
    npy, npz, jq, kb = pn.npy, pn.npz, pn.jq, pn.kb
    xt, cz, nch, nic, groups, ng = fs.xt, fs.cz, fs.nch, fs.nic, fs.groups, fs.ng
    mesh_id = pl.DeviceIdType.MESH

    def load(s, c):
        x = pl.multiple_of(lax.rem(d + 1 + s, npy) * xt, xt)
        b = lax.rem(s, 2)
        return pltpu.make_async_copy(
            v_hbm.at[:, :, pl.ds(c * cz, cz), pl.ds(x, xt)],
            vbuf.at[b, :, :, pl.ds(c * cz, cz), :], sv.at[b, c])

    for c in range(nch):
        load(0, c).start()

    barrier = pltpu.get_barrier_semaphore()
    for o in range(1, npy * npz):
        od, op = divmod(o, npz)
        to = (lax.rem(d + od, npy), lax.rem(p + op, npz))
        pl.semaphore_signal(barrier, inc=1, device_id=to, device_id_type=mesh_id)

    part[...] = jnp.zeros_like(part)
    weights(pn, fs, d, p, w2, wx)

    sub = lax.rem(lax.broadcasted_iota(jnp.int32, (groups, 9, 8, 128), 3), 32)
    m = nic * 8

    def up(b):
        return pltpu.make_async_remote_copy(
            src_ref=part.at[b, groups - 1], dst_ref=rec_h.at[b, 0], send_sem=sh.at[b, 0], recv_sem=rh.at[b, 0],
            device_id=(d, lax.rem(p + 1, npz)), device_id_type=mesh_id)

    def down(b):
        return pltpu.make_async_remote_copy(
            src_ref=part.at[b, 0], dst_ref=rec_h.at[b, 1], send_sem=sh.at[b, 1], recv_sem=rh.at[b, 1],
            device_id=(d, lax.rem(p + npz - 1, npz)), device_id_type=mesh_id)

    def across(b, n):
        return pltpu.make_async_remote_copy(
            src_ref=part.at[b, pl.ds(1, ng), :, pl.ds(0, n)], dst_ref=rec_y.at[d, :, :, pl.ds(0, n)],
            send_sem=sy.at[b], recv_sem=ry.at[b], device_id=(lax.rem(d + 1 + b, npy), p), device_id_type=mesh_id)

    def slant(b, k, n):
        o = 1 if b else 0
        to = (lax.rem(d + 1 + b, npy), lax.rem(p + (1 if k == 0 else npz - 1), npz))
        return pltpu.make_async_remote_copy(
            src_ref=part.at[b, groups - 1 if k == 0 else 0, :, pl.ds(0, n)], dst_ref=rec_d.at[o, k, :, pl.ds(0, n)],
            send_sem=sd.at[o, k], recv_sem=rd.at[o, k], device_id=to, device_id_type=mesh_id)

    def by_rows(who, act):
        for n in sorted(set(fs.sent)):
            mine = [who == i for i in range(npy) if fs.sent[i] == n]

            @pl.when(functools.reduce(jnp.logical_or, mine))
            def _():
                act(n)

    def halo_start(b):
        @pl.when(p < npz - 1)
        def _():
            up(b).start()

        @pl.when(p > 0)
        def _():
            down(b).start()

    def halo_finish(b):
        @pl.when(p > 0)
        def _():
            up(b).wait_recv()
            part[b, 1] += rec_h[b, 0]

        @pl.when(p < npz - 1)
        def _():
            down(b).wait_recv()
            part[b, ng] += rec_h[b, 1]

    def halo_sent(b):
        @pl.when(p < npz - 1)
        def _():
            up(b).wait_send()

        @pl.when(p > 0)
        def _():
            down(b).wait_send()

    def block(s, carry):
        b = lax.rem(s, 2)

        @pl.when(s < npy - 1)
        def _():
            for c in range(nch):
                load(s + 1, c).start()

        acc[...] = jnp.zeros_like(acc)
        for c in range(nch):
            load(s, c).wait()
            wt = w2[c].astype(bf16)
            row = fs.first[0] + fs.step * p + c * (cz // 8)
            for f in range(9):
                if f < 3:
                    val = vbuf[b, f, :, c * cz:(c + 1) * cz, :]
                else:
                    a1, a2 = stress_pairs[f - 3]
                    val = vbuf[b, a1, :, c * cz:(c + 1) * cz, :] * vbuf[b, a2, :, c * cz:(c + 1) * cz, :]
                hi, lo = split(val.reshape(fs.kk, xt))
                if f % 2 == 0:
                    r = dot(wt, hi)
                    r = r[:m] + r[m:] + dot(wt[:m], lo)
                else:
                    r_lo = dot(wt[:m], lo)
                    r = dot(wt, hi)
                    r = r[:m] + r[m:] + r_lo
                acc[f, pl.ds(row, nic)] += r.reshape(nic, 8, xt)

        left, right = lax.rem(s + npy - 1, npy), lax.rem(s + 1, npy)
        res = None
        for h in range(2):
            cols = []
            for q in (2 * h, 2 * h + 1):
                a = jnp.concatenate([acc[f, 4 * g + q] for g in range(groups) for f in range(9)], axis=0)
                hi, lo = split(a)
                cols += [hi, lo, hi]
            r = dot(jnp.concatenate(cols, axis=1), wx[6 * xt * h:6 * xt * (h + 1)])
            res = r if res is None else res + r
        main = res[:, :128].reshape(groups, 9, 8, 128)
        edge = res[:, 128:].reshape(groups, 9, 8, 128)
        part[s] += main
        part[left] += jnp.where(sub >= 16, edge, 0.0)
        part[right] += jnp.where(sub < 16, edge, 0.0)

        @pl.when(s == 1)
        def _():
            pl.semaphore_wait(barrier, npy * npz - 1)

        @pl.when(s >= 3)
        def _():
            halo_finish(s - 2)
            by_rows(d, lambda n: across(s - 2, n).start())

        @pl.when((s >= 2) & (s <= npy - 2))
        def _():
            halo_start(s - 1)
        return carry

    lax.fori_loop(0, npy, block, 0)
    own = npy - 1
    has_up, has_down = p < npz - 1, p > 0

    def late_start(n):
        for b in (npy - 2, 0):
            across(b, n).start()
            for k in range(2):
                @pl.when((has_up, has_down)[k])
                def _():
                    slant(b, k, n).start()

    by_rows(d, late_start)
    halo_start(own)
    halo_finish(own)
    rec_y[d] = part[own, 1:1 + ng]
    for b in list(range(1, npy - 1)) + [0]:
        src = lax.rem(d + 2 * npy - 1 - b, npy)

        def arrive(n):
            across(b, n).wait_recv()
            if b in (npy - 2, 0):
                for k in range(2):
                    @pl.when((has_down, has_up)[k])
                    def _():
                        slant(b, k, n).wait_recv()
                        rec_y[src, 0 if k == 0 else ng - 1] += rec_d[1 if b else 0, k]

        by_rows(src, arrive)

    tot[...] = jnp.zeros_like(tot)
    for s in range(npy):
        j, n = fs.jlo[s], fs.rows[s]
        tot[:, :, j:j + n, :] += rec_y[s, :, :, 0:n, :]
    for q in range(npz):
        snd_z[q] = tot[:, :, q * jq:(q + 1) * jq, :]
    copies = []
    for o in range(1, npz):
        to = lax.rem(p + o, npz)
        copy = pltpu.make_async_remote_copy(
            src_ref=snd_z.at[to], dst_ref=rec_z.at[p], send_sem=sz.at[o], recv_sem=rz.at[o],
            device_id=(d, to), device_id_type=mesh_id)
        copy.start()
        copies.append(copy)
    rec_z[p] = snd_z[p]
    for copy in copies:
        copy.wait()
    for b in list(range(1, npy - 2)) + [own]:
        halo_sent(b)

    def sent(n):
        for b in range(npy - 1):
            across(b, n).wait_send()
        for b in (npy - 2, 0):
            for k in range(2):
                @pl.when((has_up, has_down)[k])
                def _():
                    slant(b, k, n).wait_send()

    by_rows(d, sent)
    for s in range(npz):
        for g in range(ng):
            t = rec_z[s, g]
            tau = [t[3 + n] - t[a] * t[b] for n, (a, b) in enumerate(stress_pairs)]
            for q in range(4):
                i = fs.own * s + 4 * g + q
                for n in range(3):
                    vel_ref[n, i] = t[n, :, q * kb:(q + 1) * kb]
                for n in range(6):
                    str_ref[n, i] = tau[n][:, q * kb:(q + 1) * kb]


def fused(pn, fs, velocity):
    vmem = pl.BlockSpec(memory_space=pltpu.VMEM)
    hbm = pl.BlockSpec(memory_space=pltpu.HBM)
    npy, npz, ng = pn.npy, pn.npz, fs.ng
    dma = lambda *n: pltpu.SemaphoreType.DMA(n)
    return pl.pallas_call(
        functools.partial(fused_kernel, pn, fs),
        in_specs=[hbm],
        out_specs=(vmem, vmem),
        out_shape=tuple(jax.ShapeDtypeStruct((n, pn.oz, pn.jq, pn.kb), f32) for n in (3, 6)),
        scratch_shapes=[
            pltpu.VMEM((2, 3, pn.yl, pn.zl, fs.xt), f32),
            pltpu.VMEM((12 * fs.xt, 256), bf16),
            pltpu.VMEM((fs.nch, 2 * fs.nic * 8, fs.kk), f32),
            pltpu.VMEM((9, fs.slots, 8, fs.xt), f32),
            pltpu.VMEM((npy, fs.groups, 9, 8, 128), f32),
            pltpu.VMEM((npy, 2, 9, 8, 128), f32),
            pltpu.VMEM((2, 2, 9, 8, 128), f32),
            pltpu.VMEM((npy, ng, 9, 8, 128), f32),
            pltpu.VMEM((ng, 9, pn.oy, 128), f32),
            pltpu.VMEM((npz, ng, 9, pn.jq, 128), f32),
            pltpu.VMEM((npz, ng, 9, pn.jq, 128), f32),
            dma(2, fs.nch), dma(npy, 2), dma(npy, 2), dma(2, 2), dma(2, 2), dma(npy), dma(npy), dma(npz), dma(npz),
        ],
        compiler_params=pltpu.CompilerParams(
            collective_id=0, has_side_effects=True, vmem_limit_bytes=50 * 2**20
        ),
    )(velocity)


def on_device(npy, npz, velocity):
    pn = Plan(velocity.shape, npy, npz)
    fs = Fast(pn)
    v = jnp.transpose(velocity, (0, 2, 1, 3))
    if fs.ok:
        return fused(pn, fs, v)
    return exchange(pn, local_sums(pn, v))


def solution(mesh):
    return jax.shard_map(
        functools.partial(on_device, mesh.shape["py"], mesh.shape["pz"]),
        mesh=mesh,
        in_specs=(P(None, "pz", "py", None),),
        out_specs=(P(None, None, "pz", "py"), P(None, None, "pz", "py")),
        check_vma=False,
    )
```

```python
import functools
import numpy as np
import ml_dtypes
import jax
import jax.numpy as jnp
from jax import lax
from jax.sharding import PartitionSpec as P
from jax.experimental import pallas as pl
from jax.experimental.pallas import tpu as pltpu

stress_pairs = ((0, 0), (0, 1), (0, 2), (1, 1), (1, 2), (2, 2))
f32, bf16 = jnp.float32, jnp.bfloat16


def tap(t):
    r = np.arange(-16, 17).astype(np.float64)
    s = np.sum(np.exp(-r * r / 128.0))
    t = np.asarray(t, np.float64)
    return np.where(np.abs(t) <= 16, np.exp(-t * t / 128.0) / s, 0.0)


class Plan:
    def __init__(self, shape, npy, npz):
        _, self.zl, self.yl, self.nx = shape
        self.npy, self.npz = npy, npz
        zl, yl = self.zl, self.yl
        self.oz = (zl * npz - 32) // 8
        self.oy = (yl * npy - 32) // 8
        self.ox = self.nx // 8
        self.kb = self.ox // npy
        self.jq = self.oy // npz
        self.pk = 128 // self.kb
        self.cz = 8 if zl % 8 == 0 else zl
        self.nch = zl // self.cz
        self.zp = -(-self.cz // 8) * 8
        self.kk = yl * self.zp
        cz, nch = self.cz, self.nch
        base = lambda s: (s + 7) // 8 - 4
        self.base_p = [base(zl * p) for p in range(npz)]
        starts = np.array([[zl * p + cz * c for c in range(nch)] for p in range(npz)])
        bases = base(starts)
        self.nic = int(np.max((starts + cz - 1) // 8 - bases + 1))
        self.offs = bases - bases[:, :1]
        self.ni = int(self.offs.max()) + self.nic
        self.groups = -(-self.ni // self.pk)
        z = starts[:, :, None, None] + np.arange(cz)[None, None, None, :]
        i = bases[:, :, None, None] + np.arange(8)[None, None, :, None]
        az = np.where((i >= 0) & (i < self.oz), tap(z - 16 - 8 * i), 0.0)
        az[:, :, self.nic:] = 0.0
        az = np.pad(az, ((0, 0), (0, 0), (0, 0), (0, self.zp - cz)))
        self.az = np.tile(az, (1, 1, 1, yl)).astype(np.float32)
        ay = np.zeros((npy, 8, yl))
        self.mask = np.zeros((npy, self.oy // 8, 8), np.float32)
        for d in range(npy):
            y = yl * d + np.arange(yl)
            for j in range(self.oy):
                w = tap(y - 16 - 8 * j)
                if np.any(w != 0):
                    ay[d, j % 8] += w
                    self.mask[d, j // 8, j % 8] = 1.0
        assert self.mask.sum(axis=1).max() == 1
        self.ay = np.repeat(ay, self.zp, axis=2).astype(np.float32)
        n = np.arange(self.nx)[:, None]
        k = np.arange(self.ox)[None, :]
        t = (n - 8 * k + self.nx // 2) % self.nx - self.nx // 2
        wx = tap(t).astype(np.float32)
        self.wx_hi = wx.astype(ml_dtypes.bfloat16)
        self.wx_lo = (wx - self.wx_hi.astype(np.float32)).astype(ml_dtypes.bfloat16)


def split(val):
    hi = val.astype(bf16)
    return hi, (val - hi.astype(f32)).astype(bf16)


def dot(a, b):
    return jnp.dot(a, b, preferred_element_type=f32)


def sum_block(pn, c, p, d, v_ref, az_ref, ay_ref, acc):
    xt = 512
    wz = az_ref[p, c][: pn.nic]
    wy = ay_ref[d]
    w = (wz[:, None, :] * wy[None, :, :]).reshape(pn.nic * 8, pn.kk)
    w_hi = w.astype(bf16).astype(f32)
    w2 = jnp.concatenate([w_hi, w - w_hi], axis=0).astype(bf16)
    off = (pn.zl * p + pn.cz * c + 7) // 8 - (pn.zl * p + 7) // 8
    m = pn.nic * 8

    def tile(x, carry):
        xs = pl.ds(pl.multiple_of(x * xt, xt), xt)
        comps = []
        for a in range(3):
            blk = v_ref[a, :, :, xs]
            if pn.zp > pn.cz:
                blk = jnp.concatenate([blk, jnp.zeros((pn.yl, pn.zp - pn.cz, xt), f32)], axis=1)
            comps.append(blk.reshape(pn.kk, xt))
        for f in range(9):
            if f < 3:
                val = comps[f]
            else:
                a, b = stress_pairs[f - 3]
                val = comps[a] * comps[b]
            hi, lo = split(val)
            r = dot(w2, hi) + dot(w2, lo)
            r = (r[:m] + r[m:]).reshape(pn.nic, 8, xt)
            acc[f, pl.ds(off, pn.nic), :, xs] += r
        return carry

    lax.fori_loop(0, pn.nx // xt, tile, 0)


def first_group(pn, g, acc, wh_ref, wl_ref, out_ref):
    rows = min(pn.pk, pn.ni - g * pn.pk)
    parts = []
    for q in range(rows):
        a = acc[:, g * pn.pk + q].reshape(72, pn.nx)
        hi, lo = split(a)
        parts.append(dot(hi, wh_ref[...]) + (dot(lo, wh_ref[...]) + dot(hi, wl_ref[...])))
    lane = lax.broadcasted_iota(jnp.int32, (72, 128), 1)
    for m in range(pn.npy):
        mg, mo = divmod(m * pn.kb, 128)
        res = jnp.zeros((72, 128), f32)
        for q in range(rows):
            piece = parts[q][:, mg * 128:(mg + 1) * 128]
            shift = (q * pn.kb - mo) % 128
            if shift:
                piece = pltpu.roll(piece, shift, 1)
            res = jnp.where((lane >= q * pn.kb) & (lane < (q + 1) * pn.kb), piece, res)
        out_ref[m, g] = res.reshape(9, 8, 128)


def local_kernel(pn, v_ref, az_ref, ay_ref, wh_ref, wl_ref, out_ref, acc):
    c = pl.program_id(0)
    d, p = lax.axis_index("py"), lax.axis_index("pz")

    @pl.when(c == 0)
    def _():
        acc[...] = jnp.zeros_like(acc)

    sum_block(pn, c, p, d, v_ref, az_ref, ay_ref, acc)

    @pl.when(c == pn.nch - 1)
    def _():
        for g in range(pn.groups):
            first_group(pn, g, acc, wh_ref, wl_ref, out_ref)


def local_sums(pn, velocity):
    whole = lambda a: pl.BlockSpec(a.shape, lambda c: (0,) * a.ndim)
    tables = [pn.az, pn.ay, pn.wx_hi, pn.wx_lo]
    return pl.pallas_call(
        functools.partial(local_kernel, pn),
        grid=(pn.nch,),
        in_specs=[pl.BlockSpec((3, pn.yl, pn.cz, pn.nx), lambda c: (0, 0, c, 0))] + [whole(t) for t in tables],
        out_specs=pl.BlockSpec((pn.npy, pn.groups, 9, 8, 128), lambda c: (0, 0, 0, 0, 0)),
        out_shape=jax.ShapeDtypeStruct((pn.npy, pn.groups, 9, 8, 128), f32),
        scratch_shapes=[pltpu.VMEM((9, pn.ni, 8, pn.nx), f32)],
        compiler_params=pltpu.CompilerParams(vmem_limit_bytes=50 * 2**20),
    )(velocity, *[jnp.asarray(t) for t in tables])


def exchange_kernel(pn, in_ref, vel_ref, str_ref, rec_y, snd_z, rec_z, sy, ry, sz, rz):
    d, p = lax.axis_index("py"), lax.axis_index("pz")
    npy, npz, jq, kb = pn.npy, pn.npz, pn.jq, pn.kb
    mesh_id = pl.DeviceIdType.MESH
    barrier = pltpu.get_barrier_semaphore()
    for o in range(1, npy):
        pl.semaphore_signal(barrier, inc=1, device_id=(lax.rem(d + o, npy), p), device_id_type=mesh_id)
    for o in range(1, npz):
        pl.semaphore_signal(barrier, inc=1, device_id=(d, lax.rem(p + o, npz)), device_id_type=mesh_id)
    pl.semaphore_wait(barrier, npy + npz - 2)

    y_copies = []
    for g in range(pn.groups):
        y_copies.append([])
        for o in range(1, npy):
            to = lax.rem(d + o, npy)
            copy = pltpu.make_async_remote_copy(
                src_ref=in_ref.at[to, g], dst_ref=rec_y.at[d, g], send_sem=sy.at[g, o], recv_sem=ry.at[g, o],
                device_id=(to, p), device_id_type=mesh_id)
            copy.start()
            y_copies[g].append(copy)
    rec_y[d] = in_ref[d]
    z_copies = []

    row = lax.broadcasted_iota(jnp.int32, (9, 8, 128), 1)
    for g in range(pn.groups):
        for copy in y_copies[g]:
            copy.wait()
        for h in range(pn.oy // 8):
            total = jnp.zeros((9, 8, 128), f32)
            for s in range(npy):
                rows = np.nonzero(pn.mask[s, h])[0]
                if len(rows) == 0:
                    continue
                val = rec_y[s, g]
                if len(rows) < 8:
                    val = jnp.where((row >= int(rows[0])) & (row <= int(rows[-1])), val, 0.0)
                total = total + val
            for part in range(8 // jq):
                snd_z[h * (8 // jq) + part, g] = total[:, part * jq:(part + 1) * jq, :]
        for o in range(1, npz):
            to = lax.rem(p + o, npz)
            copy = pltpu.make_async_remote_copy(
                src_ref=snd_z.at[to, g], dst_ref=rec_z.at[p, g], send_sem=sz.at[g, o], recv_sem=rz.at[g, o],
                device_id=(d, to), device_id_type=mesh_id)
            copy.start()
            z_copies.append(copy)
    rec_z[p] = snd_z[p]
    for copy in z_copies:
        copy.wait()

    for i in range(pn.oz):
        total = jnp.zeros((9, jq, kb), f32)
        for s in range(npz):
            n = i - pn.base_p[s]
            if 0 <= n < pn.ni:
                g, q = divmod(n, pn.pk)
                total = total + rec_z[s, g, :, :, q * kb:(q + 1) * kb]
        vel_ref[:, i] = total[:3]
        for n, (a, b) in enumerate(stress_pairs):
            str_ref[n, i] = total[3 + n] - total[a] * total[b]


def exchange(pn, packed):
    vmem = pl.BlockSpec(memory_space=pltpu.VMEM)
    zbuf = pltpu.VMEM((pn.npz, pn.groups, 9, pn.jq, 128), f32)
    sems = [pltpu.SemaphoreType.DMA((pn.groups, n)) for n in (pn.npy, pn.npy, pn.npz, pn.npz)]
    return pl.pallas_call(
        functools.partial(exchange_kernel, pn),
        in_specs=[vmem],
        out_specs=(vmem, vmem),
        out_shape=tuple(jax.ShapeDtypeStruct((n, pn.oz, pn.jq, pn.kb), f32) for n in (3, 6)),
        scratch_shapes=[pltpu.VMEM((pn.npy, pn.groups, 9, 8, 128), f32), zbuf, zbuf] + sems,
        compiler_params=pltpu.CompilerParams(
            collective_id=0, has_side_effects=True, vmem_limit_bytes=32 * 2**20
        ),
    )(packed)


class Fast:
    def __init__(self, pn):
        self.npy, self.npz = pn.npy, pn.npz
        npy, npz = pn.npy, pn.npz
        self.xt = pn.nx // npy
        self.kb = pn.kb
        self.own = pn.oz // npz
        self.ok = pn.kb == 32 and pn.oz % npz == 0 and self.own % 4 == 0 and pn.oy % 8 == 0 and pn.oy % npz == 0
        self.ok = self.ok and pn.jq in (4, 8) and npy >= 4 and npz >= 2 and pn.zl % 8 == 0 and pn.mask.sum(axis=1).max() == 1
        if not self.ok:
            return
        self.cz = next(c for c in (24, 16, 8) if pn.zl % c == 0)
        self.nch = pn.zl // self.cz
        self.kk = pn.yl * self.cz
        self.nic = (self.cz - 1) // 8 + 5
        self.groups = self.own // 4 + 2
        self.ng = self.own // 4
        self.slots = self.groups * 4
        first = [(pn.zl * p) // 8 - 4 - (self.own * p - 4) for p in range(npz)]
        self.first = first
        self.step = first[1] - first[0]
        self.ok = all(f == first[0] + self.step * p for p, f in enumerate(first))
        y0 = pn.yl * np.arange(npy)
        self.jlo = [int(max(0, (y + 7) // 8 - 4)) for y in y0]
        self.rows = [int(min(pn.oy - 1, (y + pn.yl - 1) // 8)) - j + 1 for y, j in zip(y0, self.jlo)]
        self.sent = [min(8, n | 1) for n in self.rows]
        self.ok = self.ok and 0 < min(self.rows) and max(self.rows) <= 8 and min(first) >= 0 and max(first) + (self.nch - 1) * self.cz // 8 + self.nic <= self.slots
        if not self.ok:
            return


def taps(t):
    r = np.arange(-16, 17).astype(np.float64)
    scale = float(1.0 / np.sum(np.exp(-r * r / 128.0)))
    val = jnp.exp((t * t).astype(f32) * (-1.0 / 128.0)) * scale
    return jnp.where((t >= -16) & (t <= 16), val, 0.0)


def weights(pn, fs, d, p, w2, wx):
    iota = lax.broadcasted_iota
    nic, cz, xt = fs.nic, fs.cz, fs.xt
    m = nic * 8
    col = iota(jnp.int32, (8, fs.kk), 1)
    slot = iota(jnp.int32, (8, fs.kk), 0)
    y = jnp.floor((col.astype(f32) + 0.5) * (1.0 / cz)).astype(jnp.int32)
    z = col - y * cz
    j = jnp.maximum((pn.yl * d + 7) // 8 - 4, 0) + slot
    wy = jnp.where(j < pn.oy, taps(pn.yl * d + y - 16 - 8 * j), 0.0)
    wz0 = taps(z + 16 - 8 * slot)
    for c in range(fs.nch):
        i = (pn.zl * p + cz * c) // 8 - 4 + slot
        wz = jnp.where((i >= 0) & (i < pn.oz), wz0, 0.0)[:nic]
        w = (wz[:, None, :] * wy[None, :, :]).reshape(m, fs.kk)
        w_hi = w.astype(bf16).astype(f32)
        w2[c, :m] = w_hi
        w2[c, m:] = w - w_hi
    row = iota(jnp.int32, (xt, 128), 0)
    lane = iota(jnp.int32, (xt, 128), 1)
    k = lane & 31
    t = row - 8 * k
    main = taps(t)
    edge = taps(jnp.where(k >= 16, t + xt, t - xt))
    for q in range(4):
        here = (lane >> 5) == q
        val = jnp.concatenate([jnp.where(here, main, 0.0), jnp.where(here, edge, 0.0)], axis=1)
        hi, lo = split(val)
        for n, part in enumerate((hi, hi, lo)):
            wx[(3 * q + n) * xt:(3 * q + n + 1) * xt] = part


def fused_kernel(pn, fs, v_hbm, vel_ref, str_ref,
                 vbuf, wx, w2, acc, part, rec_h, rec_d, rec_y, tot, snd_z, rec_z,
                 sv, sh, rh, sd, rd, sy, ry, sz, rz):
    d, p = lax.axis_index("py"), lax.axis_index("pz")
    npy, npz, jq, kb = pn.npy, pn.npz, pn.jq, pn.kb
    xt, cz, nch, nic, groups, ng = fs.xt, fs.cz, fs.nch, fs.nic, fs.groups, fs.ng
    mesh_id = pl.DeviceIdType.MESH

    def load(s, c):
        x = pl.multiple_of(lax.rem(d + 1 + s, npy) * xt, xt)
        b = lax.rem(s, 2)
        return pltpu.make_async_copy(
            v_hbm.at[:, :, pl.ds(c * cz, cz), pl.ds(x, xt)],
            vbuf.at[b, :, :, pl.ds(c * cz, cz), :], sv.at[b, c])

    for c in range(nch):
        load(0, c).start()

    barrier = pltpu.get_barrier_semaphore()
    for o in range(1, npy * npz):
        od, op = divmod(o, npz)
        to = (lax.rem(d + od, npy), lax.rem(p + op, npz))
        pl.semaphore_signal(barrier, inc=1, device_id=to, device_id_type=mesh_id)

    part[...] = jnp.zeros_like(part)
    weights(pn, fs, d, p, w2, wx)

    sub = lax.rem(lax.broadcasted_iota(jnp.int32, (groups, 9, 8, 128), 3), 32)
    m = nic * 8

    def up(b):
        return pltpu.make_async_remote_copy(
            src_ref=part.at[b, groups - 1], dst_ref=rec_h.at[b, 0], send_sem=sh.at[b, 0], recv_sem=rh.at[b, 0],
            device_id=(d, lax.rem(p + 1, npz)), device_id_type=mesh_id)

    def down(b):
        return pltpu.make_async_remote_copy(
            src_ref=part.at[b, 0], dst_ref=rec_h.at[b, 1], send_sem=sh.at[b, 1], recv_sem=rh.at[b, 1],
            device_id=(d, lax.rem(p + npz - 1, npz)), device_id_type=mesh_id)

    def across(b, n):
        return pltpu.make_async_remote_copy(
            src_ref=part.at[b, pl.ds(1, ng), :, pl.ds(0, n)], dst_ref=rec_y.at[d, :, :, pl.ds(0, n)],
            send_sem=sy.at[b], recv_sem=ry.at[b], device_id=(lax.rem(d + 1 + b, npy), p), device_id_type=mesh_id)

    def slant(b, k, n):
        o = 1 if b else 0
        to = (lax.rem(d + 1 + b, npy), lax.rem(p + (1 if k == 0 else npz - 1), npz))
        return pltpu.make_async_remote_copy(
            src_ref=part.at[b, groups - 1 if k == 0 else 0, :, pl.ds(0, n)], dst_ref=rec_d.at[o, k, :, pl.ds(0, n)],
            send_sem=sd.at[o, k], recv_sem=rd.at[o, k], device_id=to, device_id_type=mesh_id)

    def by_rows(who, act):
        for n in sorted(set(fs.sent)):
            mine = [who == i for i in range(npy) if fs.sent[i] == n]

            @pl.when(functools.reduce(jnp.logical_or, mine))
            def _():
                act(n)

    def halo_start(b):
        @pl.when(p < npz - 1)
        def _():
            up(b).start()

        @pl.when(p > 0)
        def _():
            down(b).start()

    def halo_finish(b):
        @pl.when(p > 0)
        def _():
            up(b).wait_recv()
            part[b, 1] += rec_h[b, 0]

        @pl.when(p < npz - 1)
        def _():
            down(b).wait_recv()
            part[b, ng] += rec_h[b, 1]

    def halo_sent(b):
        @pl.when(p < npz - 1)
        def _():
            up(b).wait_send()

        @pl.when(p > 0)
        def _():
            down(b).wait_send()

    def block(s, carry):
        b = lax.rem(s, 2)

        @pl.when(s < npy - 1)
        def _():
            for c in range(nch):
                load(s + 1, c).start()

        acc[...] = jnp.zeros_like(acc)
        for c in range(nch):
            load(s, c).wait()
            wt = w2[c].astype(bf16)
            row = fs.first[0] + fs.step * p + c * (cz // 8)
            for n, f in enumerate((0, 3, 4, 1, 6, 7, 2, 8, 5)):
                if f < 3:
                    val = vbuf[b, f, :, c * cz:(c + 1) * cz, :]
                else:
                    a1, a2 = stress_pairs[f - 3]
                    val = vbuf[b, a1, :, c * cz:(c + 1) * cz, :] * vbuf[b, a2, :, c * cz:(c + 1) * cz, :]
                hi, lo = split(val.reshape(fs.kk, xt))
                if n % 2 == 0:
                    r = dot(wt, hi)
                    r = r[:m] + r[m:] + dot(wt[:m], lo)
                else:
                    r_lo = dot(wt[:m], lo)
                    r = dot(wt, hi)
                    r = r[:m] + r[m:] + r_lo
                acc[f, pl.ds(row, nic)] += r.reshape(nic, 8, xt)

        left, right = lax.rem(s + npy - 1, npy), lax.rem(s + 1, npy)
        res = None
        for h in range(2):
            cols = []
            for q in (2 * h, 2 * h + 1):
                a = jnp.concatenate([acc[f, 4 * g + q] for g in range(groups) for f in range(9)], axis=0)
                hi, lo = split(a)
                cols += [hi, lo, hi]
            r = dot(jnp.concatenate(cols, axis=1), wx[6 * xt * h:6 * xt * (h + 1)])
            res = r if res is None else res + r
        main = res[:, :128].reshape(groups, 9, 8, 128)
        edge = res[:, 128:].reshape(groups, 9, 8, 128)
        part[s] += main
        part[left] += jnp.where(sub >= 16, edge, 0.0)
        part[right] += jnp.where(sub < 16, edge, 0.0)

        @pl.when(s == 1)
        def _():
            pl.semaphore_wait(barrier, npy * npz - 1)

        @pl.when(s >= 3)
        def _():
            halo_finish(s - 2)
            by_rows(d, lambda n: across(s - 2, n).start())

        @pl.when((s >= 2) & (s <= npy - 2))
        def _():
            halo_start(s - 1)
        return carry

    lax.fori_loop(0, npy, block, 0)
    own = npy - 1
    has_up, has_down = p < npz - 1, p > 0

    def late_start(n):
        for b in (npy - 2, 0):
            across(b, n).start()
            for k in range(2):
                @pl.when((has_up, has_down)[k])
                def _():
                    slant(b, k, n).start()

    by_rows(d, late_start)
    halo_start(own)
    halo_finish(own)
    rec_y[d] = part[own, 1:1 + ng]
    for b in list(range(1, npy - 1)) + [0]:
        src = lax.rem(d + 2 * npy - 1 - b, npy)

        def arrive(n):
            across(b, n).wait_recv()
            if b in (npy - 2, 0):
                for k in range(2):
                    @pl.when((has_down, has_up)[k])
                    def _():
                        slant(b, k, n).wait_recv()
                        rec_y[src, 0 if k == 0 else ng - 1] += rec_d[1 if b else 0, k]

        by_rows(src, arrive)

    tot[...] = jnp.zeros_like(tot)
    for s in range(npy):
        j, n = fs.jlo[s], fs.rows[s]
        tot[:, :, j:j + n, :] += rec_y[s, :, :, 0:n, :]
    for q in range(npz):
        snd_z[q] = tot[:, :, q * jq:(q + 1) * jq, :]
    copies = []
    for o in range(1, npz):
        to = lax.rem(p + o, npz)
        copy = pltpu.make_async_remote_copy(
            src_ref=snd_z.at[to], dst_ref=rec_z.at[p], send_sem=sz.at[o], recv_sem=rz.at[o],
            device_id=(d, to), device_id_type=mesh_id)
        copy.start()
        copies.append(copy)
    rec_z[p] = snd_z[p]
    for copy in copies:
        copy.wait()
    for b in list(range(1, npy - 2)) + [own]:
        halo_sent(b)

    def sent(n):
        for b in range(npy - 1):
            across(b, n).wait_send()
        for b in (npy - 2, 0):
            for k in range(2):
                @pl.when((has_up, has_down)[k])
                def _():
                    slant(b, k, n).wait_send()

    by_rows(d, sent)
    for s in range(npz):
        for g in range(ng):
            t = rec_z[s, g]
            tau = [t[3 + n] - t[a] * t[b] for n, (a, b) in enumerate(stress_pairs)]
            for q in range(4):
                i = fs.own * s + 4 * g + q
                for n in range(3):
                    vel_ref[n, i] = t[n, :, q * kb:(q + 1) * kb]
                for n in range(6):
                    str_ref[n, i] = tau[n][:, q * kb:(q + 1) * kb]


def fused(pn, fs, velocity):
    vmem = pl.BlockSpec(memory_space=pltpu.VMEM)
    hbm = pl.BlockSpec(memory_space=pltpu.HBM)
    npy, npz, ng = pn.npy, pn.npz, fs.ng
    dma = lambda *n: pltpu.SemaphoreType.DMA(n)
    return pl.pallas_call(
        functools.partial(fused_kernel, pn, fs),
        in_specs=[hbm],
        out_specs=(vmem, vmem),
        out_shape=tuple(jax.ShapeDtypeStruct((n, pn.oz, pn.jq, pn.kb), f32) for n in (3, 6)),
        scratch_shapes=[
            pltpu.VMEM((2, 3, pn.yl, pn.zl, fs.xt), f32),
            pltpu.VMEM((12 * fs.xt, 256), bf16),
            pltpu.VMEM((fs.nch, 2 * fs.nic * 8, fs.kk), f32),
            pltpu.VMEM((9, fs.slots, 8, fs.xt), f32),
            pltpu.VMEM((npy, fs.groups, 9, 8, 128), f32),
            pltpu.VMEM((npy, 2, 9, 8, 128), f32),
            pltpu.VMEM((2, 2, 9, 8, 128), f32),
            pltpu.VMEM((npy, ng, 9, 8, 128), f32),
            pltpu.VMEM((ng, 9, pn.oy, 128), f32),
            pltpu.VMEM((npz, ng, 9, pn.jq, 128), f32),
            pltpu.VMEM((npz, ng, 9, pn.jq, 128), f32),
            dma(2, fs.nch), dma(npy, 2), dma(npy, 2), dma(2, 2), dma(2, 2), dma(npy), dma(npy), dma(npz), dma(npz),
        ],
        compiler_params=pltpu.CompilerParams(
            collective_id=0, has_side_effects=True, vmem_limit_bytes=50 * 2**20
        ),
    )(velocity)


def on_device(npy, npz, velocity):
    pn = Plan(velocity.shape, npy, npz)
    fs = Fast(pn)
    v = jnp.transpose(velocity, (0, 2, 1, 3))
    if fs.ok:
        return fused(pn, fs, v)
    return exchange(pn, local_sums(pn, v))


def solution(mesh):
    return jax.shard_map(
        functools.partial(on_device, mesh.shape["py"], mesh.shape["pz"]),
        mesh=mesh,
        in_specs=(P(None, "pz", "py", None),),
        out_specs=(P(None, None, "pz", "py"), P(None, None, "pz", "py")),
        check_vma=False,
    )
```

```python
import functools
import numpy as np
import ml_dtypes
import jax
import jax.numpy as jnp
from jax import lax
from jax.sharding import PartitionSpec as P
from jax.experimental import pallas as pl
from jax.experimental.pallas import tpu as pltpu

stress_pairs = ((0, 0), (0, 1), (0, 2), (1, 1), (1, 2), (2, 2))
f32, bf16 = jnp.float32, jnp.bfloat16


def tap(t):
    r = np.arange(-16, 17).astype(np.float64)
    s = np.sum(np.exp(-r * r / 128.0))
    t = np.asarray(t, np.float64)
    return np.where(np.abs(t) <= 16, np.exp(-t * t / 128.0) / s, 0.0)


class Plan:
    def __init__(self, shape, npy, npz):
        _, self.zl, self.yl, self.nx = shape
        self.npy, self.npz = npy, npz
        zl, yl = self.zl, self.yl
        self.oz = (zl * npz - 32) // 8
        self.oy = (yl * npy - 32) // 8
        self.ox = self.nx // 8
        self.kb = self.ox // npy
        self.jq = self.oy // npz
        self.pk = 128 // self.kb
        self.cz = 8 if zl % 8 == 0 else zl
        self.nch = zl // self.cz
        self.zp = -(-self.cz // 8) * 8
        self.kk = yl * self.zp
        cz, nch = self.cz, self.nch
        base = lambda s: (s + 7) // 8 - 4
        self.base_p = [base(zl * p) for p in range(npz)]
        starts = np.array([[zl * p + cz * c for c in range(nch)] for p in range(npz)])
        bases = base(starts)
        self.nic = int(np.max((starts + cz - 1) // 8 - bases + 1))
        self.offs = bases - bases[:, :1]
        self.ni = int(self.offs.max()) + self.nic
        self.groups = -(-self.ni // self.pk)
        z = starts[:, :, None, None] + np.arange(cz)[None, None, None, :]
        i = bases[:, :, None, None] + np.arange(8)[None, None, :, None]
        az = np.where((i >= 0) & (i < self.oz), tap(z - 16 - 8 * i), 0.0)
        az[:, :, self.nic:] = 0.0
        az = np.pad(az, ((0, 0), (0, 0), (0, 0), (0, self.zp - cz)))
        self.az = np.tile(az, (1, 1, 1, yl)).astype(np.float32)
        ay = np.zeros((npy, 8, yl))
        self.mask = np.zeros((npy, self.oy // 8, 8), np.float32)
        for d in range(npy):
            y = yl * d + np.arange(yl)
            for j in range(self.oy):
                w = tap(y - 16 - 8 * j)
                if np.any(w != 0):
                    ay[d, j % 8] += w
                    self.mask[d, j // 8, j % 8] = 1.0
        assert self.mask.sum(axis=1).max() == 1
        self.ay = np.repeat(ay, self.zp, axis=2).astype(np.float32)
        n = np.arange(self.nx)[:, None]
        k = np.arange(self.ox)[None, :]
        t = (n - 8 * k + self.nx // 2) % self.nx - self.nx // 2
        wx = tap(t).astype(np.float32)
        self.wx_hi = wx.astype(ml_dtypes.bfloat16)
        self.wx_lo = (wx - self.wx_hi.astype(np.float32)).astype(ml_dtypes.bfloat16)


def split(val):
    hi = val.astype(bf16)
    return hi, (val - hi.astype(f32)).astype(bf16)


def dot(a, b):
    return jnp.dot(a, b, preferred_element_type=f32)


def sum_block(pn, c, p, d, v_ref, az_ref, ay_ref, acc):
    xt = 512
    wz = az_ref[p, c][: pn.nic]
    wy = ay_ref[d]
    w = (wz[:, None, :] * wy[None, :, :]).reshape(pn.nic * 8, pn.kk)
    w_hi = w.astype(bf16).astype(f32)
    w2 = jnp.concatenate([w_hi, w - w_hi], axis=0).astype(bf16)
    off = (pn.zl * p + pn.cz * c + 7) // 8 - (pn.zl * p + 7) // 8
    m = pn.nic * 8

    def tile(x, carry):
        xs = pl.ds(pl.multiple_of(x * xt, xt), xt)
        comps = []
        for a in range(3):
            blk = v_ref[a, :, :, xs]
            if pn.zp > pn.cz:
                blk = jnp.concatenate([blk, jnp.zeros((pn.yl, pn.zp - pn.cz, xt), f32)], axis=1)
            comps.append(blk.reshape(pn.kk, xt))
        for f in range(9):
            if f < 3:
                val = comps[f]
            else:
                a, b = stress_pairs[f - 3]
                val = comps[a] * comps[b]
            hi, lo = split(val)
            r = dot(w2, hi) + dot(w2, lo)
            r = (r[:m] + r[m:]).reshape(pn.nic, 8, xt)
            acc[f, pl.ds(off, pn.nic), :, xs] += r
        return carry

    lax.fori_loop(0, pn.nx // xt, tile, 0)


def first_group(pn, g, acc, wh_ref, wl_ref, out_ref):
    rows = min(pn.pk, pn.ni - g * pn.pk)
    parts = []
    for q in range(rows):
        a = acc[:, g * pn.pk + q].reshape(72, pn.nx)
        hi, lo = split(a)
        parts.append(dot(hi, wh_ref[...]) + (dot(lo, wh_ref[...]) + dot(hi, wl_ref[...])))
    lane = lax.broadcasted_iota(jnp.int32, (72, 128), 1)
    for m in range(pn.npy):
        mg, mo = divmod(m * pn.kb, 128)
        res = jnp.zeros((72, 128), f32)
        for q in range(rows):
            piece = parts[q][:, mg * 128:(mg + 1) * 128]
            shift = (q * pn.kb - mo) % 128
            if shift:
                piece = pltpu.roll(piece, shift, 1)
            res = jnp.where((lane >= q * pn.kb) & (lane < (q + 1) * pn.kb), piece, res)
        out_ref[m, g] = res.reshape(9, 8, 128)


def local_kernel(pn, v_ref, az_ref, ay_ref, wh_ref, wl_ref, out_ref, acc):
    c = pl.program_id(0)
    d, p = lax.axis_index("py"), lax.axis_index("pz")

    @pl.when(c == 0)
    def _():
        acc[...] = jnp.zeros_like(acc)

    sum_block(pn, c, p, d, v_ref, az_ref, ay_ref, acc)

    @pl.when(c == pn.nch - 1)
    def _():
        for g in range(pn.groups):
            first_group(pn, g, acc, wh_ref, wl_ref, out_ref)


def local_sums(pn, velocity):
    whole = lambda a: pl.BlockSpec(a.shape, lambda c: (0,) * a.ndim)
    tables = [pn.az, pn.ay, pn.wx_hi, pn.wx_lo]
    return pl.pallas_call(
        functools.partial(local_kernel, pn),
        grid=(pn.nch,),
        in_specs=[pl.BlockSpec((3, pn.yl, pn.cz, pn.nx), lambda c: (0, 0, c, 0))] + [whole(t) for t in tables],
        out_specs=pl.BlockSpec((pn.npy, pn.groups, 9, 8, 128), lambda c: (0, 0, 0, 0, 0)),
        out_shape=jax.ShapeDtypeStruct((pn.npy, pn.groups, 9, 8, 128), f32),
        scratch_shapes=[pltpu.VMEM((9, pn.ni, 8, pn.nx), f32)],
        compiler_params=pltpu.CompilerParams(vmem_limit_bytes=50 * 2**20),
    )(velocity, *[jnp.asarray(t) for t in tables])


def exchange_kernel(pn, in_ref, vel_ref, str_ref, rec_y, snd_z, rec_z, sy, ry, sz, rz):
    d, p = lax.axis_index("py"), lax.axis_index("pz")
    npy, npz, jq, kb = pn.npy, pn.npz, pn.jq, pn.kb
    mesh_id = pl.DeviceIdType.MESH
    barrier = pltpu.get_barrier_semaphore()
    for o in range(1, npy):
        pl.semaphore_signal(barrier, inc=1, device_id=(lax.rem(d + o, npy), p), device_id_type=mesh_id)
    for o in range(1, npz):
        pl.semaphore_signal(barrier, inc=1, device_id=(d, lax.rem(p + o, npz)), device_id_type=mesh_id)
    pl.semaphore_wait(barrier, npy + npz - 2)

    y_copies = []
    for g in range(pn.groups):
        y_copies.append([])
        for o in range(1, npy):
            to = lax.rem(d + o, npy)
            copy = pltpu.make_async_remote_copy(
                src_ref=in_ref.at[to, g], dst_ref=rec_y.at[d, g], send_sem=sy.at[g, o], recv_sem=ry.at[g, o],
                device_id=(to, p), device_id_type=mesh_id)
            copy.start()
            y_copies[g].append(copy)
    rec_y[d] = in_ref[d]
    z_copies = []

    row = lax.broadcasted_iota(jnp.int32, (9, 8, 128), 1)
    for g in range(pn.groups):
        for copy in y_copies[g]:
            copy.wait()
        for h in range(pn.oy // 8):
            total = jnp.zeros((9, 8, 128), f32)
            for s in range(npy):
                rows = np.nonzero(pn.mask[s, h])[0]
                if len(rows) == 0:
                    continue
                val = rec_y[s, g]
                if len(rows) < 8:
                    val = jnp.where((row >= int(rows[0])) & (row <= int(rows[-1])), val, 0.0)
                total = total + val
            for part in range(8 // jq):
                snd_z[h * (8 // jq) + part, g] = total[:, part * jq:(part + 1) * jq, :]
        for o in range(1, npz):
            to = lax.rem(p + o, npz)
            copy = pltpu.make_async_remote_copy(
                src_ref=snd_z.at[to, g], dst_ref=rec_z.at[p, g], send_sem=sz.at[g, o], recv_sem=rz.at[g, o],
                device_id=(d, to), device_id_type=mesh_id)
            copy.start()
            z_copies.append(copy)
    rec_z[p] = snd_z[p]
    for copy in z_copies:
        copy.wait()

    for i in range(pn.oz):
        total = jnp.zeros((9, jq, kb), f32)
        for s in range(npz):
            n = i - pn.base_p[s]
            if 0 <= n < pn.ni:
                g, q = divmod(n, pn.pk)
                total = total + rec_z[s, g, :, :, q * kb:(q + 1) * kb]
        vel_ref[:, i] = total[:3]
        for n, (a, b) in enumerate(stress_pairs):
            str_ref[n, i] = total[3 + n] - total[a] * total[b]


def exchange(pn, packed):
    vmem = pl.BlockSpec(memory_space=pltpu.VMEM)
    zbuf = pltpu.VMEM((pn.npz, pn.groups, 9, pn.jq, 128), f32)
    sems = [pltpu.SemaphoreType.DMA((pn.groups, n)) for n in (pn.npy, pn.npy, pn.npz, pn.npz)]
    return pl.pallas_call(
        functools.partial(exchange_kernel, pn),
        in_specs=[vmem],
        out_specs=(vmem, vmem),
        out_shape=tuple(jax.ShapeDtypeStruct((n, pn.oz, pn.jq, pn.kb), f32) for n in (3, 6)),
        scratch_shapes=[pltpu.VMEM((pn.npy, pn.groups, 9, 8, 128), f32), zbuf, zbuf] + sems,
        compiler_params=pltpu.CompilerParams(
            collective_id=0, has_side_effects=True, vmem_limit_bytes=32 * 2**20
        ),
    )(packed)


class Fast:
    def __init__(self, pn):
        self.npy, self.npz = pn.npy, pn.npz
        npy, npz = pn.npy, pn.npz
        self.xt = pn.nx // npy
        self.kb = pn.kb
        self.own = pn.oz // npz
        self.ok = pn.kb == 32 and pn.oz % npz == 0 and self.own % 4 == 0 and pn.oy % 8 == 0 and pn.oy % npz == 0
        self.ok = self.ok and pn.jq in (4, 8) and npy >= 4 and npz >= 2 and pn.zl % 8 == 0 and pn.mask.sum(axis=1).max() == 1
        if not self.ok:
            return
        self.cz = next(c for c in (24, 16, 8) if pn.zl % c == 0)
        self.nch = pn.zl // self.cz
        self.kk = pn.yl * self.cz
        self.nic = (self.cz - 1) // 8 + 5
        self.groups = self.own // 4 + 2
        self.ng = self.own // 4
        self.slots = self.groups * 4
        first = [(pn.zl * p) // 8 - 4 - (self.own * p - 4) for p in range(npz)]
        self.first = first
        self.step = first[1] - first[0]
        self.ok = all(f == first[0] + self.step * p for p, f in enumerate(first))
        y0 = pn.yl * np.arange(npy)
        self.jlo = [int(max(0, (y + 7) // 8 - 4)) for y in y0]
        self.rows = [int(min(pn.oy - 1, (y + pn.yl - 1) // 8)) - j + 1 for y, j in zip(y0, self.jlo)]
        self.sent = [min(8, n | 1) for n in self.rows]
        self.ok = self.ok and 0 < min(self.rows) and max(self.rows) <= 8 and min(first) >= 0 and max(first) + (self.nch - 1) * self.cz // 8 + self.nic <= self.slots
        if not self.ok:
            return


def taps(t):
    r = np.arange(-16, 17).astype(np.float64)
    scale = float(1.0 / np.sum(np.exp(-r * r / 128.0)))
    val = jnp.exp((t * t).astype(f32) * (-1.0 / 128.0)) * scale
    return jnp.where((t >= -16) & (t <= 16), val, 0.0)


def weights(pn, fs, d, p, w2, w1, wx):
    iota = lax.broadcasted_iota
    nic, cz, xt = fs.nic, fs.cz, fs.xt
    m = nic * 8
    col = iota(jnp.int32, (8, fs.kk), 1)
    slot = iota(jnp.int32, (8, fs.kk), 0)
    y = jnp.floor((col.astype(f32) + 0.5) * (1.0 / cz)).astype(jnp.int32)
    z = col - y * cz
    j = jnp.maximum((pn.yl * d + 7) // 8 - 4, 0) + slot
    wy = jnp.where(j < pn.oy, taps(pn.yl * d + y - 16 - 8 * j), 0.0)
    wz0 = taps(z + 16 - 8 * slot)
    for c in range(fs.nch):
        i = (pn.zl * p + cz * c) // 8 - 4 + slot
        wz = jnp.where((i >= 0) & (i < pn.oz), wz0, 0.0)[:nic]
        w = (wz[:, None, :] * wy[None, :, :]).reshape(m, fs.kk)
        w_hi = w.astype(bf16).astype(f32)
        w2[c] = jnp.concatenate([w_hi, w - w_hi], axis=0).astype(bf16)
        w1[c] = jnp.concatenate([w_hi, jnp.zeros((w1.shape[1] - m, fs.kk), f32)], axis=0).astype(bf16)
    row = iota(jnp.int32, (xt, 128), 0)
    lane = iota(jnp.int32, (xt, 128), 1)
    k = lane & 31
    t = row - 8 * k
    main = taps(t)
    edge = taps(jnp.where(k >= 16, t + xt, t - xt))
    for q in range(4):
        here = (lane >> 5) == q
        val = jnp.concatenate([jnp.where(here, main, 0.0), jnp.where(here, edge, 0.0)], axis=1)
        hi, lo = split(val)
        for n, part in enumerate((hi, hi, lo)):
            wx[(3 * q + n) * xt:(3 * q + n + 1) * xt] = part


def fused_kernel(pn, fs, v_hbm, vel_ref, str_ref,
                 vbuf, wx, w2, w1, acc, part, rec_h, rec_d, rec_y, tot, snd_z, rec_z,
                 sv, sh, rh, sd, rd, sy, ry, sz, rz):
    d, p = lax.axis_index("py"), lax.axis_index("pz")
    npy, npz, jq, kb = pn.npy, pn.npz, pn.jq, pn.kb
    xt, cz, nch, nic, groups, ng = fs.xt, fs.cz, fs.nch, fs.nic, fs.groups, fs.ng
    mesh_id = pl.DeviceIdType.MESH

    def load(s, c):
        x = pl.multiple_of(lax.rem(d + 1 + s, npy) * xt, xt)
        b = lax.rem(s, 2)
        return pltpu.make_async_copy(
            v_hbm.at[:, :, pl.ds(c * cz, cz), pl.ds(x, xt)],
            vbuf.at[b, :, :, pl.ds(c * cz, cz), :], sv.at[b, c])

    for c in range(nch):
        load(0, c).start()

    barrier = pltpu.get_barrier_semaphore()
    for o in range(1, npy * npz):
        od, op = divmod(o, npz)
        to = (lax.rem(d + od, npy), lax.rem(p + op, npz))
        pl.semaphore_signal(barrier, inc=1, device_id=to, device_id_type=mesh_id)

    part[...] = jnp.zeros_like(part)
    weights(pn, fs, d, p, w2, w1, wx)

    sub = lax.rem(lax.broadcasted_iota(jnp.int32, (groups, 9, 8, 128), 3), 32)
    m = nic * 8

    def up(b):
        return pltpu.make_async_remote_copy(
            src_ref=part.at[b, groups - 1], dst_ref=rec_h.at[b, 0], send_sem=sh.at[b, 0], recv_sem=rh.at[b, 0],
            device_id=(d, lax.rem(p + 1, npz)), device_id_type=mesh_id)

    def down(b):
        return pltpu.make_async_remote_copy(
            src_ref=part.at[b, 0], dst_ref=rec_h.at[b, 1], send_sem=sh.at[b, 1], recv_sem=rh.at[b, 1],
            device_id=(d, lax.rem(p + npz - 1, npz)), device_id_type=mesh_id)

    def across(b, n):
        return pltpu.make_async_remote_copy(
            src_ref=part.at[b, pl.ds(1, ng), :, pl.ds(0, n)], dst_ref=rec_y.at[d, :, :, pl.ds(0, n)],
            send_sem=sy.at[b], recv_sem=ry.at[b], device_id=(lax.rem(d + 1 + b, npy), p), device_id_type=mesh_id)

    def slant(b, k, n):
        o = 1 if b else 0
        to = (lax.rem(d + 1 + b, npy), lax.rem(p + (1 if k == 0 else npz - 1), npz))
        return pltpu.make_async_remote_copy(
            src_ref=part.at[b, groups - 1 if k == 0 else 0, :, pl.ds(0, n)], dst_ref=rec_d.at[o, k, :, pl.ds(0, n)],
            send_sem=sd.at[o, k], recv_sem=rd.at[o, k], device_id=to, device_id_type=mesh_id)

    def by_rows(who, act):
        for n in sorted(set(fs.sent)):
            mine = [who == i for i in range(npy) if fs.sent[i] == n]

            @pl.when(functools.reduce(jnp.logical_or, mine))
            def _():
                act(n)

    def halo_start(b):
        @pl.when(p < npz - 1)
        def _():
            up(b).start()

        @pl.when(p > 0)
        def _():
            down(b).start()

    def halo_finish(b):
        @pl.when(p > 0)
        def _():
            up(b).wait_recv()
            part[b, 1] += rec_h[b, 0]

        @pl.when(p < npz - 1)
        def _():
            down(b).wait_recv()
            part[b, ng] += rec_h[b, 1]

    def halo_sent(b):
        @pl.when(p < npz - 1)
        def _():
            up(b).wait_send()

        @pl.when(p > 0)
        def _():
            down(b).wait_send()

    def block(s, carry):
        b = lax.rem(s, 2)

        @pl.when(s < npy - 1)
        def _():
            for c in range(nch):
                load(s + 1, c).start()

        acc[...] = jnp.zeros_like(acc)
        for c in range(nch):
            load(s, c).wait()
            wt, wt_hi = w2[c], w1[c]
            row = fs.first[0] + fs.step * p + c * (cz // 8)
            for n, f in enumerate((0, 3, 4, 1, 6, 7, 2, 8, 5)):
                if f < 3:
                    val = vbuf[b, f, :, c * cz:(c + 1) * cz, :]
                else:
                    a1, a2 = stress_pairs[f - 3]
                    val = vbuf[b, a1, :, c * cz:(c + 1) * cz, :] * vbuf[b, a2, :, c * cz:(c + 1) * cz, :]
                hi, lo = split(val.reshape(fs.kk, xt))
                if (n + c) % 2 == 0:
                    r = dot(wt, hi)
                    r = r[:m] + r[m:] + dot(wt_hi, lo)[:m]
                else:
                    r_lo = dot(wt_hi, lo)[:m]
                    r = dot(wt, hi)
                    r = r[:m] + r[m:] + r_lo
                acc[f, pl.ds(row, nic)] += r.reshape(nic, 8, xt)

        left, right = lax.rem(s + npy - 1, npy), lax.rem(s + 1, npy)
        res = None
        for h in range(2):
            cols = []
            for q in (2 * h, 2 * h + 1):
                a = jnp.concatenate([acc[f, 4 * g + q] for g in range(groups) for f in range(9)], axis=0)
                hi, lo = split(a)
                cols += [hi, lo, hi]
            r = dot(jnp.concatenate(cols, axis=1), wx[6 * xt * h:6 * xt * (h + 1)])
            res = r if res is None else res + r
        main = res[:, :128].reshape(groups, 9, 8, 128)
        edge = res[:, 128:].reshape(groups, 9, 8, 128)
        part[s] += main
        part[left] += jnp.where(sub >= 16, edge, 0.0)
        part[right] += jnp.where(sub < 16, edge, 0.0)

        @pl.when(s == 1)
        def _():
            pl.semaphore_wait(barrier, npy * npz - 1)

        @pl.when(s >= 3)
        def _():
            halo_finish(s - 2)
            by_rows(d, lambda n: across(s - 2, n).start())

        @pl.when((s >= 2) & (s <= npy - 2))
        def _():
            halo_start(s - 1)
        return carry

    lax.fori_loop(0, npy, block, 0)
    own = npy - 1
    has_up, has_down = p < npz - 1, p > 0

    def late_start(n):
        for b in (npy - 2, 0):
            across(b, n).start()
            for k in range(2):
                @pl.when((has_up, has_down)[k])
                def _():
                    slant(b, k, n).start()

    by_rows(d, late_start)
    halo_start(own)
    halo_finish(own)
    rec_y[d] = part[own, 1:1 + ng]
    for b in list(range(1, npy - 1)) + [0]:
        src = lax.rem(d + 2 * npy - 1 - b, npy)

        def arrive(n):
            across(b, n).wait_recv()
            if b in (npy - 2, 0):
                for k in range(2):
                    @pl.when((has_down, has_up)[k])
                    def _():
                        slant(b, k, n).wait_recv()
                        rec_y[src, 0 if k == 0 else ng - 1] += rec_d[1 if b else 0, k]

        by_rows(src, arrive)

    tot[...] = jnp.zeros_like(tot)
    for s in range(npy):
        j, n = fs.jlo[s], fs.rows[s]
        tot[:, :, j:j + n, :] += rec_y[s, :, :, 0:n, :]
    for q in range(npz):
        snd_z[q] = tot[:, :, q * jq:(q + 1) * jq, :]
    copies = []
    for o in range(1, npz):
        to = lax.rem(p + o, npz)
        copy = pltpu.make_async_remote_copy(
            src_ref=snd_z.at[to], dst_ref=rec_z.at[p], send_sem=sz.at[o], recv_sem=rz.at[o],
            device_id=(d, to), device_id_type=mesh_id)
        copy.start()
        copies.append(copy)
    rec_z[p] = snd_z[p]
    for copy in copies:
        copy.wait()
    for b in list(range(1, npy - 2)) + [own]:
        halo_sent(b)

    def sent(n):
        for b in range(npy - 1):
            across(b, n).wait_send()
        for b in (npy - 2, 0):
            for k in range(2):
                @pl.when((has_up, has_down)[k])
                def _():
                    slant(b, k, n).wait_send()

    by_rows(d, sent)
    for s in range(npz):
        for g in range(ng):
            t = rec_z[s, g]
            tau = [t[3 + n] - t[a] * t[b] for n, (a, b) in enumerate(stress_pairs)]
            for q in range(4):
                i = fs.own * s + 4 * g + q
                for n in range(3):
                    vel_ref[n, i] = t[n, :, q * kb:(q + 1) * kb]
                for n in range(6):
                    str_ref[n, i] = tau[n][:, q * kb:(q + 1) * kb]


def fused(pn, fs, velocity):
    vmem = pl.BlockSpec(memory_space=pltpu.VMEM)
    hbm = pl.BlockSpec(memory_space=pltpu.HBM)
    npy, npz, ng = pn.npy, pn.npz, fs.ng
    dma = lambda *n: pltpu.SemaphoreType.DMA(n)
    return pl.pallas_call(
        functools.partial(fused_kernel, pn, fs),
        in_specs=[hbm],
        out_specs=(vmem, vmem),
        out_shape=tuple(jax.ShapeDtypeStruct((n, pn.oz, pn.jq, pn.kb), f32) for n in (3, 6)),
        scratch_shapes=[
            pltpu.VMEM((2, 3, pn.yl, pn.zl, fs.xt), f32),
            pltpu.VMEM((12 * fs.xt, 256), bf16),
            pltpu.VMEM((fs.nch, 2 * fs.nic * 8, fs.kk), bf16),
            pltpu.VMEM((fs.nch, -(-fs.nic // 2) * 16, fs.kk), bf16),
            pltpu.VMEM((9, fs.slots, 8, fs.xt), f32),
            pltpu.VMEM((npy, fs.groups, 9, 8, 128), f32),
            pltpu.VMEM((npy, 2, 9, 8, 128), f32),
            pltpu.VMEM((2, 2, 9, 8, 128), f32),
            pltpu.VMEM((npy, ng, 9, 8, 128), f32),
            pltpu.VMEM((ng, 9, pn.oy, 128), f32),
            pltpu.VMEM((npz, ng, 9, pn.jq, 128), f32),
            pltpu.VMEM((npz, ng, 9, pn.jq, 128), f32),
            dma(2, fs.nch), dma(npy, 2), dma(npy, 2), dma(2, 2), dma(2, 2), dma(npy), dma(npy), dma(npz), dma(npz),
        ],
        compiler_params=pltpu.CompilerParams(
            collective_id=0, has_side_effects=True, vmem_limit_bytes=50 * 2**20
        ),
    )(velocity)


def on_device(npy, npz, velocity):
    pn = Plan(velocity.shape, npy, npz)
    fs = Fast(pn)
    v = jnp.transpose(velocity, (0, 2, 1, 3))
    if fs.ok:
        return fused(pn, fs, v)
    return exchange(pn, local_sums(pn, v))


def solution(mesh):
    return jax.shard_map(
        functools.partial(on_device, mesh.shape["py"], mesh.shape["pz"]),
        mesh=mesh,
        in_specs=(P(None, "pz", "py", None),),
        out_specs=(P(None, None, "pz", "py"), P(None, None, "pz", "py")),
        check_vma=False,
    )
```

```python
import functools
import numpy as np
import ml_dtypes
import jax
import jax.numpy as jnp
from jax import lax
from jax.sharding import PartitionSpec as P
from jax.experimental import pallas as pl
from jax.experimental.pallas import tpu as pltpu

stress_pairs = ((0, 0), (0, 1), (0, 2), (1, 1), (1, 2), (2, 2))
f32, bf16 = jnp.float32, jnp.bfloat16


def tap(t):
    r = np.arange(-16, 17).astype(np.float64)
    s = np.sum(np.exp(-r * r / 128.0))
    t = np.asarray(t, np.float64)
    return np.where(np.abs(t) <= 16, np.exp(-t * t / 128.0) / s, 0.0)


class Plan:
    def __init__(self, shape, npy, npz):
        _, self.zl, self.yl, self.nx = shape
        self.npy, self.npz = npy, npz
        zl, yl = self.zl, self.yl
        self.oz = (zl * npz - 32) // 8
        self.oy = (yl * npy - 32) // 8
        self.ox = self.nx // 8
        self.kb = self.ox // npy
        self.jq = self.oy // npz
        self.pk = 128 // self.kb
        self.cz = 8 if zl % 8 == 0 else zl
        self.nch = zl // self.cz
        self.zp = -(-self.cz // 8) * 8
        self.kk = yl * self.zp
        cz, nch = self.cz, self.nch
        base = lambda s: (s + 7) // 8 - 4
        self.base_p = [base(zl * p) for p in range(npz)]
        starts = np.array([[zl * p + cz * c for c in range(nch)] for p in range(npz)])
        bases = base(starts)
        self.nic = int(np.max((starts + cz - 1) // 8 - bases + 1))
        self.offs = bases - bases[:, :1]
        self.ni = int(self.offs.max()) + self.nic
        self.groups = -(-self.ni // self.pk)
        z = starts[:, :, None, None] + np.arange(cz)[None, None, None, :]
        i = bases[:, :, None, None] + np.arange(8)[None, None, :, None]
        az = np.where((i >= 0) & (i < self.oz), tap(z - 16 - 8 * i), 0.0)
        az[:, :, self.nic:] = 0.0
        az = np.pad(az, ((0, 0), (0, 0), (0, 0), (0, self.zp - cz)))
        self.az = np.tile(az, (1, 1, 1, yl)).astype(np.float32)
        ay = np.zeros((npy, 8, yl))
        self.mask = np.zeros((npy, self.oy // 8, 8), np.float32)
        for d in range(npy):
            y = yl * d + np.arange(yl)
            for j in range(self.oy):
                w = tap(y - 16 - 8 * j)
                if np.any(w != 0):
                    ay[d, j % 8] += w
                    self.mask[d, j // 8, j % 8] = 1.0
        assert self.mask.sum(axis=1).max() == 1
        self.ay = np.repeat(ay, self.zp, axis=2).astype(np.float32)
        n = np.arange(self.nx)[:, None]
        k = np.arange(self.ox)[None, :]
        t = (n - 8 * k + self.nx // 2) % self.nx - self.nx // 2
        wx = tap(t).astype(np.float32)
        self.wx_hi = wx.astype(ml_dtypes.bfloat16)
        self.wx_lo = (wx - self.wx_hi.astype(np.float32)).astype(ml_dtypes.bfloat16)


def split(val):
    hi = val.astype(bf16)
    return hi, (val - hi.astype(f32)).astype(bf16)


def dot(a, b):
    return jnp.dot(a, b, preferred_element_type=f32)


def sum_block(pn, c, p, d, v_ref, az_ref, ay_ref, acc):
    xt = 512
    wz = az_ref[p, c][: pn.nic]
    wy = ay_ref[d]
    w = (wz[:, None, :] * wy[None, :, :]).reshape(pn.nic * 8, pn.kk)
    w_hi = w.astype(bf16).astype(f32)
    w2 = jnp.concatenate([w_hi, w - w_hi], axis=0).astype(bf16)
    off = (pn.zl * p + pn.cz * c + 7) // 8 - (pn.zl * p + 7) // 8
    m = pn.nic * 8

    def tile(x, carry):
        xs = pl.ds(pl.multiple_of(x * xt, xt), xt)
        comps = []
        for a in range(3):
            blk = v_ref[a, :, :, xs]
            if pn.zp > pn.cz:
                blk = jnp.concatenate([blk, jnp.zeros((pn.yl, pn.zp - pn.cz, xt), f32)], axis=1)
            comps.append(blk.reshape(pn.kk, xt))
        for f in range(9):
            if f < 3:
                val = comps[f]
            else:
                a, b = stress_pairs[f - 3]
                val = comps[a] * comps[b]
            hi, lo = split(val)
            r = dot(w2, hi) + dot(w2, lo)
            r = (r[:m] + r[m:]).reshape(pn.nic, 8, xt)
            acc[f, pl.ds(off, pn.nic), :, xs] += r
        return carry

    lax.fori_loop(0, pn.nx // xt, tile, 0)


def first_group(pn, g, acc, wh_ref, wl_ref, out_ref):
    rows = min(pn.pk, pn.ni - g * pn.pk)
    parts = []
    for q in range(rows):
        a = acc[:, g * pn.pk + q].reshape(72, pn.nx)
        hi, lo = split(a)
        parts.append(dot(hi, wh_ref[...]) + (dot(lo, wh_ref[...]) + dot(hi, wl_ref[...])))
    lane = lax.broadcasted_iota(jnp.int32, (72, 128), 1)
    for m in range(pn.npy):
        mg, mo = divmod(m * pn.kb, 128)
        res = jnp.zeros((72, 128), f32)
        for q in range(rows):
            piece = parts[q][:, mg * 128:(mg + 1) * 128]
            shift = (q * pn.kb - mo) % 128
            if shift:
                piece = pltpu.roll(piece, shift, 1)
            res = jnp.where((lane >= q * pn.kb) & (lane < (q + 1) * pn.kb), piece, res)
        out_ref[m, g] = res.reshape(9, 8, 128)


def local_kernel(pn, v_ref, az_ref, ay_ref, wh_ref, wl_ref, out_ref, acc):
    c = pl.program_id(0)
    d, p = lax.axis_index("py"), lax.axis_index("pz")

    @pl.when(c == 0)
    def _():
        acc[...] = jnp.zeros_like(acc)

    sum_block(pn, c, p, d, v_ref, az_ref, ay_ref, acc)

    @pl.when(c == pn.nch - 1)
    def _():
        for g in range(pn.groups):
            first_group(pn, g, acc, wh_ref, wl_ref, out_ref)


def local_sums(pn, velocity):
    whole = lambda a: pl.BlockSpec(a.shape, lambda c: (0,) * a.ndim)
    tables = [pn.az, pn.ay, pn.wx_hi, pn.wx_lo]
    return pl.pallas_call(
        functools.partial(local_kernel, pn),
        grid=(pn.nch,),
        in_specs=[pl.BlockSpec((3, pn.yl, pn.cz, pn.nx), lambda c: (0, 0, c, 0))] + [whole(t) for t in tables],
        out_specs=pl.BlockSpec((pn.npy, pn.groups, 9, 8, 128), lambda c: (0, 0, 0, 0, 0)),
        out_shape=jax.ShapeDtypeStruct((pn.npy, pn.groups, 9, 8, 128), f32),
        scratch_shapes=[pltpu.VMEM((9, pn.ni, 8, pn.nx), f32)],
        compiler_params=pltpu.CompilerParams(vmem_limit_bytes=50 * 2**20),
    )(velocity, *[jnp.asarray(t) for t in tables])


def exchange_kernel(pn, in_ref, vel_ref, str_ref, rec_y, snd_z, rec_z, sy, ry, sz, rz):
    d, p = lax.axis_index("py"), lax.axis_index("pz")
    npy, npz, jq, kb = pn.npy, pn.npz, pn.jq, pn.kb
    mesh_id = pl.DeviceIdType.MESH
    barrier = pltpu.get_barrier_semaphore()
    for o in range(1, npy):
        pl.semaphore_signal(barrier, inc=1, device_id=(lax.rem(d + o, npy), p), device_id_type=mesh_id)
    for o in range(1, npz):
        pl.semaphore_signal(barrier, inc=1, device_id=(d, lax.rem(p + o, npz)), device_id_type=mesh_id)
    pl.semaphore_wait(barrier, npy + npz - 2)

    y_copies = []
    for g in range(pn.groups):
        y_copies.append([])
        for o in range(1, npy):
            to = lax.rem(d + o, npy)
            copy = pltpu.make_async_remote_copy(
                src_ref=in_ref.at[to, g], dst_ref=rec_y.at[d, g], send_sem=sy.at[g, o], recv_sem=ry.at[g, o],
                device_id=(to, p), device_id_type=mesh_id)
            copy.start()
            y_copies[g].append(copy)
    rec_y[d] = in_ref[d]
    z_copies = []

    row = lax.broadcasted_iota(jnp.int32, (9, 8, 128), 1)
    for g in range(pn.groups):
        for copy in y_copies[g]:
            copy.wait()
        for h in range(pn.oy // 8):
            total = jnp.zeros((9, 8, 128), f32)
            for s in range(npy):
                rows = np.nonzero(pn.mask[s, h])[0]
                if len(rows) == 0:
                    continue
                val = rec_y[s, g]
                if len(rows) < 8:
                    val = jnp.where((row >= int(rows[0])) & (row <= int(rows[-1])), val, 0.0)
                total = total + val
            for part in range(8 // jq):
                snd_z[h * (8 // jq) + part, g] = total[:, part * jq:(part + 1) * jq, :]
        for o in range(1, npz):
            to = lax.rem(p + o, npz)
            copy = pltpu.make_async_remote_copy(
                src_ref=snd_z.at[to, g], dst_ref=rec_z.at[p, g], send_sem=sz.at[g, o], recv_sem=rz.at[g, o],
                device_id=(d, to), device_id_type=mesh_id)
            copy.start()
            z_copies.append(copy)
    rec_z[p] = snd_z[p]
    for copy in z_copies:
        copy.wait()

    for i in range(pn.oz):
        total = jnp.zeros((9, jq, kb), f32)
        for s in range(npz):
            n = i - pn.base_p[s]
            if 0 <= n < pn.ni:
                g, q = divmod(n, pn.pk)
                total = total + rec_z[s, g, :, :, q * kb:(q + 1) * kb]
        vel_ref[:, i] = total[:3]
        for n, (a, b) in enumerate(stress_pairs):
            str_ref[n, i] = total[3 + n] - total[a] * total[b]


def exchange(pn, packed):
    vmem = pl.BlockSpec(memory_space=pltpu.VMEM)
    zbuf = pltpu.VMEM((pn.npz, pn.groups, 9, pn.jq, 128), f32)
    sems = [pltpu.SemaphoreType.DMA((pn.groups, n)) for n in (pn.npy, pn.npy, pn.npz, pn.npz)]
    return pl.pallas_call(
        functools.partial(exchange_kernel, pn),
        in_specs=[vmem],
        out_specs=(vmem, vmem),
        out_shape=tuple(jax.ShapeDtypeStruct((n, pn.oz, pn.jq, pn.kb), f32) for n in (3, 6)),
        scratch_shapes=[pltpu.VMEM((pn.npy, pn.groups, 9, 8, 128), f32), zbuf, zbuf] + sems,
        compiler_params=pltpu.CompilerParams(
            collective_id=0, has_side_effects=True, vmem_limit_bytes=32 * 2**20
        ),
    )(packed)


class Fast:
    def __init__(self, pn):
        self.npy, self.npz = pn.npy, pn.npz
        npy, npz = pn.npy, pn.npz
        self.xt = pn.nx // npy
        self.kb = pn.kb
        self.own = pn.oz // npz
        self.ok = pn.kb == 32 and pn.oz % npz == 0 and self.own % 4 == 0 and pn.oy % 8 == 0 and pn.oy % npz == 0
        self.ok = self.ok and pn.jq in (4, 8) and npy >= 4 and npz >= 2 and pn.zl % 8 == 0 and pn.mask.sum(axis=1).max() == 1
        if not self.ok:
            return
        self.cz = next(c for c in (24, 16, 8) if pn.zl % c == 0)
        self.nch = pn.zl // self.cz
        self.kk = pn.yl * self.cz
        self.nic = (self.cz - 1) // 8 + 5
        self.groups = self.own // 4 + 2
        self.ng = self.own // 4
        self.slots = self.groups * 4
        first = [(pn.zl * p) // 8 - 4 - (self.own * p - 4) for p in range(npz)]
        self.first = first
        self.step = first[1] - first[0]
        self.ok = all(f == first[0] + self.step * p for p, f in enumerate(first))
        y0 = pn.yl * np.arange(npy)
        self.jlo = [int(max(0, (y + 7) // 8 - 4)) for y in y0]
        self.rows = [int(min(pn.oy - 1, (y + pn.yl - 1) // 8)) - j + 1 for y, j in zip(y0, self.jlo)]
        self.sent = list(self.rows)
        self.ok = self.ok and 0 < min(self.rows) and max(self.rows) <= 8 and min(first) >= 0 and max(first) + (self.nch - 1) * self.cz // 8 + self.nic <= self.slots
        if not self.ok:
            return


def taps(t):
    r = np.arange(-16, 17).astype(np.float64)
    scale = float(1.0 / np.sum(np.exp(-r * r / 128.0)))
    val = jnp.exp((t * t).astype(f32) * (-1.0 / 128.0)) * scale
    return jnp.where((t >= -16) & (t <= 16), val, 0.0)


def weights(pn, fs, d, p, w2, wx):
    iota = lax.broadcasted_iota
    nic, cz, xt = fs.nic, fs.cz, fs.xt
    m = nic * 8
    col = iota(jnp.int32, (8, fs.kk), 1)
    slot = iota(jnp.int32, (8, fs.kk), 0)
    y = jnp.floor((col.astype(f32) + 0.5) * (1.0 / cz)).astype(jnp.int32)
    z = col - y * cz
    j = jnp.maximum((pn.yl * d + 7) // 8 - 4, 0) + slot
    wy = jnp.where(j < pn.oy, taps(pn.yl * d + y - 16 - 8 * j), 0.0)
    wz0 = taps(z + 16 - 8 * slot)
    for c in range(fs.nch):
        i = (pn.zl * p + cz * c) // 8 - 4 + slot
        wz = jnp.where((i >= 0) & (i < pn.oz), wz0, 0.0)[:nic]
        w = (wz[:, None, :] * wy[None, :, :]).reshape(m, fs.kk)
        w_hi = w.astype(bf16).astype(f32)
        w2[c, :m] = w_hi
        w2[c, m:] = w - w_hi
    row = iota(jnp.int32, (xt, 128), 0)
    lane = iota(jnp.int32, (xt, 128), 1)
    k = lane & 31
    t = row - 8 * k
    main = taps(t)
    edge = taps(jnp.where(k >= 16, t + xt, t - xt))
    for q in range(4):
        here = (lane >> 5) == q
        val = jnp.concatenate([jnp.where(here, main, 0.0), jnp.where(here, edge, 0.0)], axis=1)
        hi, lo = split(val)
        for n, part in enumerate((hi, hi, lo)):
            wx[(3 * q + n) * xt:(3 * q + n + 1) * xt] = part


def fused_kernel(pn, fs, v_hbm, vel_ref, str_ref,
                 vbuf, wx, w2, acc, part, rec_h, rec_d, rec_y, tot, snd_z, rec_z,
                 sv, sh, rh, sd, rd, sy, ry, sz, rz):
    d, p = lax.axis_index("py"), lax.axis_index("pz")
    npy, npz, jq, kb = pn.npy, pn.npz, pn.jq, pn.kb
    xt, cz, nch, nic, groups, ng = fs.xt, fs.cz, fs.nch, fs.nic, fs.groups, fs.ng
    mesh_id = pl.DeviceIdType.MESH

    def load(s, c):
        x = pl.multiple_of(lax.rem(d + 1 + s, npy) * xt, xt)
        b = lax.rem(s, 2)
        return pltpu.make_async_copy(
            v_hbm.at[:, :, pl.ds(c * cz, cz), pl.ds(x, xt)],
            vbuf.at[b, :, :, pl.ds(c * cz, cz), :], sv.at[b, c])

    for c in range(nch):
        load(0, c).start()

    barrier = pltpu.get_barrier_semaphore()
    for o in range(1, npy * npz):
        od, op = divmod(o, npz)
        to = (lax.rem(d + od, npy), lax.rem(p + op, npz))
        pl.semaphore_signal(barrier, inc=1, device_id=to, device_id_type=mesh_id)

    part[...] = jnp.zeros_like(part)
    weights(pn, fs, d, p, w2, wx)

    sub = lax.rem(lax.broadcasted_iota(jnp.int32, (groups, 9, 8, 128), 3), 32)
    m = nic * 8

    def up(b):
        return pltpu.make_async_remote_copy(
            src_ref=part.at[b, groups - 1], dst_ref=rec_h.at[b, 0], send_sem=sh.at[b, 0], recv_sem=rh.at[b, 0],
            device_id=(d, lax.rem(p + 1, npz)), device_id_type=mesh_id)

    def down(b):
        return pltpu.make_async_remote_copy(
            src_ref=part.at[b, 0], dst_ref=rec_h.at[b, 1], send_sem=sh.at[b, 1], recv_sem=rh.at[b, 1],
            device_id=(d, lax.rem(p + npz - 1, npz)), device_id_type=mesh_id)

    def across(b, n):
        return pltpu.make_async_remote_copy(
            src_ref=part.at[b, pl.ds(1, ng), :, pl.ds(0, n)], dst_ref=rec_y.at[d, :, :, pl.ds(0, n)],
            send_sem=sy.at[b], recv_sem=ry.at[b], device_id=(lax.rem(d + 1 + b, npy), p), device_id_type=mesh_id)

    def slant(b, k, n):
        o = 1 if b else 0
        to = (lax.rem(d + 1 + b, npy), lax.rem(p + (1 if k == 0 else npz - 1), npz))
        return pltpu.make_async_remote_copy(
            src_ref=part.at[b, groups - 1 if k == 0 else 0, :, pl.ds(0, n)], dst_ref=rec_d.at[o, k, :, pl.ds(0, n)],
            send_sem=sd.at[o, k], recv_sem=rd.at[o, k], device_id=to, device_id_type=mesh_id)

    def by_rows(who, act):
        for n in sorted(set(fs.sent)):
            mine = [who == i for i in range(npy) if fs.sent[i] == n]

            @pl.when(functools.reduce(jnp.logical_or, mine))
            def _():
                act(n)

    def halo_start(b):
        @pl.when(p < npz - 1)
        def _():
            up(b).start()

        @pl.when(p > 0)
        def _():
            down(b).start()

    def halo_finish(b):
        @pl.when(p > 0)
        def _():
            up(b).wait_recv()
            part[b, 1] += rec_h[b, 0]

        @pl.when(p < npz - 1)
        def _():
            down(b).wait_recv()
            part[b, ng] += rec_h[b, 1]

    def halo_sent(b):
        @pl.when(p < npz - 1)
        def _():
            up(b).wait_send()

        @pl.when(p > 0)
        def _():
            down(b).wait_send()

    def block(s, carry):
        b = lax.rem(s, 2)

        @pl.when(s < npy - 1)
        def _():
            for c in range(nch):
                load(s + 1, c).start()

        acc[...] = jnp.zeros_like(acc)
        for c in range(nch):
            load(s, c).wait()
            wt = w2[c].astype(bf16)
            row = fs.first[0] + fs.step * p + c * (cz // 8)
            for n, f in enumerate((0, 3, 4, 1, 6, 7, 2, 8, 5)):
                if f < 3:
                    val = vbuf[b, f, :, c * cz:(c + 1) * cz, :]
                else:
                    a1, a2 = stress_pairs[f - 3]
                    val = vbuf[b, a1, :, c * cz:(c + 1) * cz, :] * vbuf[b, a2, :, c * cz:(c + 1) * cz, :]
                hi, lo = split(val.reshape(fs.kk, xt))
                if n % 2 == 0:
                    r = dot(wt, hi)
                    r = r[:m] + r[m:] + dot(wt[:m], lo)
                else:
                    r_lo = dot(wt[:m], lo)
                    r = dot(wt, hi)
                    r = r[:m] + r[m:] + r_lo
                acc[f, pl.ds(row, nic)] += r.reshape(nic, 8, xt)

        left, right = lax.rem(s + npy - 1, npy), lax.rem(s + 1, npy)
        res = None
        for h in range(2):
            cols = []
            for q in (2 * h, 2 * h + 1):
                a = jnp.concatenate([acc[f, 4 * g + q] for g in range(groups) for f in range(9)], axis=0)
                hi, lo = split(a)
                cols += [hi, lo, hi]
            r = dot(jnp.concatenate(cols, axis=1), wx[6 * xt * h:6 * xt * (h + 1)])
            res = r if res is None else res + r
        main = res[:, :128].reshape(groups, 9, 8, 128)
        edge = res[:, 128:].reshape(groups, 9, 8, 128)
        part[s] += main
        part[left] += jnp.where(sub >= 16, edge, 0.0)
        part[right] += jnp.where(sub < 16, edge, 0.0)

        @pl.when(s == 1)
        def _():
            pl.semaphore_wait(barrier, npy * npz - 1)

        @pl.when(s >= 3)
        def _():
            halo_finish(s - 2)
            by_rows(d, lambda n: across(s - 2, n).start())

        @pl.when((s >= 2) & (s <= npy - 2))
        def _():
            halo_start(s - 1)
        return carry

    lax.fori_loop(0, npy, block, 0)
    own = npy - 1
    has_up, has_down = p < npz - 1, p > 0

    def late_start(n):
        for b in (npy - 2, 0):
            across(b, n).start()
            for k in range(2):
                @pl.when((has_up, has_down)[k])
                def _():
                    slant(b, k, n).start()

    by_rows(d, late_start)
    halo_start(own)
    halo_finish(own)
    rec_y[d] = part[own, 1:1 + ng]
    for b in list(range(1, npy - 1)) + [0]:
        src = lax.rem(d + 2 * npy - 1 - b, npy)

        def arrive(n):
            across(b, n).wait_recv()
            if b in (npy - 2, 0):
                for k in range(2):
                    @pl.when((has_down, has_up)[k])
                    def _():
                        slant(b, k, n).wait_recv()
                        rec_y[src, 0 if k == 0 else ng - 1] += rec_d[1 if b else 0, k]

        by_rows(src, arrive)

    tot[...] = jnp.zeros_like(tot)
    copies = []
    for g in range(ng):
        for s in range(npy):
            j, n = fs.jlo[s], fs.rows[s]
            tot[g, :, j:j + n, :] += rec_y[s, g, :, 0:n, :]
        for q in range(npz):
            snd_z[q, g] = tot[g, :, q * jq:(q + 1) * jq, :]
        for o in range(1, npz):
            to = lax.rem(p + o, npz)
            copy = pltpu.make_async_remote_copy(
                src_ref=snd_z.at[to, g], dst_ref=rec_z.at[p, g], send_sem=sz.at[o, g], recv_sem=rz.at[o, g],
                device_id=(d, to), device_id_type=mesh_id)
            copy.start()
            copies.append(copy)
    rec_z[p] = snd_z[p]

    for b in list(range(1, npy - 2)) + [own]:
        halo_sent(b)

    def sent(n):
        for b in range(npy - 1):
            across(b, n).wait_send()
        for b in (npy - 2, 0):
            for k in range(2):
                @pl.when((has_up, has_down)[k])
                def _():
                    slant(b, k, n).wait_send()

    by_rows(d, sent)
    for g in range(ng):
        for copy in copies[g * (npz - 1):(g + 1) * (npz - 1)]:
            copy.wait()
        for s in range(npz):
            t = rec_z[s, g]
            tau = [t[3 + n] - t[a] * t[b] for n, (a, b) in enumerate(stress_pairs)]
            for q in range(4):
                i = fs.own * s + 4 * g + q
                for n in range(3):
                    vel_ref[n, i] = t[n, :, q * kb:(q + 1) * kb]
                for n in range(6):
                    str_ref[n, i] = tau[n][:, q * kb:(q + 1) * kb]


def fused(pn, fs, velocity):
    vmem = pl.BlockSpec(memory_space=pltpu.VMEM)
    hbm = pl.BlockSpec(memory_space=pltpu.HBM)
    npy, npz, ng = pn.npy, pn.npz, fs.ng
    dma = lambda *n: pltpu.SemaphoreType.DMA(n)
    return pl.pallas_call(
        functools.partial(fused_kernel, pn, fs),
        in_specs=[hbm],
        out_specs=(vmem, vmem),
        out_shape=tuple(jax.ShapeDtypeStruct((n, pn.oz, pn.jq, pn.kb), f32) for n in (3, 6)),
        scratch_shapes=[
            pltpu.VMEM((2, 3, pn.yl, pn.zl, fs.xt), f32),
            pltpu.VMEM((12 * fs.xt, 256), bf16),
            pltpu.VMEM((fs.nch, 2 * fs.nic * 8, fs.kk), f32),
            pltpu.VMEM((9, fs.slots, 8, fs.xt), f32),
            pltpu.VMEM((npy, fs.groups, 9, 8, 128), f32),
            pltpu.VMEM((npy, 2, 9, 8, 128), f32),
            pltpu.VMEM((2, 2, 9, 8, 128), f32),
            pltpu.VMEM((npy, ng, 9, 8, 128), f32),
            pltpu.VMEM((ng, 9, pn.oy, 128), f32),
            pltpu.VMEM((npz, ng, 9, pn.jq, 128), f32),
            pltpu.VMEM((npz, ng, 9, pn.jq, 128), f32),
            dma(2, fs.nch), dma(npy, 2), dma(npy, 2), dma(2, 2), dma(2, 2), dma(npy), dma(npy), dma(npz, ng), dma(npz, ng),
        ],
        compiler_params=pltpu.CompilerParams(
            collective_id=0, has_side_effects=True, vmem_limit_bytes=50 * 2**20
        ),
    )(velocity)


def on_device(npy, npz, velocity):
    pn = Plan(velocity.shape, npy, npz)
    fs = Fast(pn)
    v = jnp.transpose(velocity, (0, 2, 1, 3))
    if fs.ok:
        return fused(pn, fs, v)
    return exchange(pn, local_sums(pn, v))


def solution(mesh):
    return jax.shard_map(
        functools.partial(on_device, mesh.shape["py"], mesh.shape["pz"]),
        mesh=mesh,
        in_specs=(P(None, "pz", "py", None),),
        out_specs=(P(None, None, "pz", "py"), P(None, None, "pz", "py")),
        check_vma=False,
    )
```
